128 devices in a mesh: cand: 8 (over x_hi, z), prompt: 16 (over x_lo, y, core).
Axes of the slice: x: 4 (x_hi: 2, x_lo: 2; x = x_hi * 2 + x_lo), y: 4, z: 4, core: 2. Of those that a mesh axis runs over, the one named last changes fastest.
Arguments:
- hidden_states: bfloat16 [16, 8, 128, 4096], P('prompt', 'cand'), may hold values from -8 to 8
- proj_weight: bfloat16 [4096, 1024], P(('cand', 'prompt')), may hold values from -0.0625 to 0.0625
- bilinear: bfloat16 [1024, 1024], P(('cand', 'prompt')), may hold values from -0.005859375 to 0.005859375
- lengths: int32 [16, 8], P('prompt'), may hold values from 32 to 128, as said below
- labels: int32 [16, 28], P('prompt'), may hold values 0 or 1
Outputs:
- pair_logits: float32 [16, 8, 8], P('prompt')
- grad_proj: float32 [4096, 1024], P(('cand', 'prompt'))
- grad_bilinear: float32 [1024, 1024], P(('cand', 'prompt'))
The draws below stay inside these ranges and needn't reach their ends.
Inputs may be any that keep to these rules, and one draw needn't show every extreme that they name: `lengths`: every prompt has a candidate with all 128 rows valid.
All inputs are finite; a program needn't handle non-finite values. No bound on the sum of `labels` on one device may be relied on, other than what follows from the above.
Results may differ from the reference program's by a relative error of at most 0.0045.
Values may be sent and summed in bfloat16 or wider, within the bound.
No kernel may reach another device: no remote copies, remote signals or barrier semaphores. Data moves between devices by JAX's collectives and lax.ppermute only.
A program may use at most 128 MiB of HBM per device.

```python
import jax
import jax.numpy as jnp
import numpy as np
from jax import lax

D = 4096
HEADS = 16
HEAD_DIM = 64
ROWS = 128
DA = 1024
CANDS = 8
PROMPTS = 16
NPAIRS = 28


def draw_hidden_states(key, part):
    shape = (PROMPTS, CANDS, ROWS, D)
    values = jax.random.normal(jax.random.fold_in(key, 1), shape, jnp.float32)
    return jnp.clip(values, -8.0, 8.0).astype(jnp.bfloat16)


def draw_lengths(key, part):
    base = jax.random.randint(jax.random.fold_in(key, 11), (PROMPTS, CANDS), ROWS // 4, ROWS + 1)
    full = jax.random.randint(jax.random.fold_in(key, 12), (PROMPTS, 1), 0, CANDS)
    return jnp.where(jnp.arange(CANDS)[None, :] == full, ROWS, base).astype(jnp.int32)


def plant(drawn, own_key, low, largest):
    longest = drawn.shape.index(max(drawn.shape))
    spots = []
    for shift in (0, 1):
        where = [jax.random.randint(jax.random.fold_in(own_key, axis), (), 0, length) for axis, length in enumerate(drawn.shape)]
        where[longest] = (where[longest] + shift) % drawn.shape[longest]
        spots.append(tuple(where))
    return drawn.at[spots[0]].set(low).at[spots[1]].set(largest)


def shard_levels(stream_key, extent, pieces, low, top_value):
    gain, own = 1.0, jax.random.fold_in(stream_key, 6)
    for position, shards_of in pieces:
        heights = jnp.exp(jax.random.uniform(jax.random.fold_in(own, position), (shards_of,), jnp.float32, low / len(pieces), top_value / len(pieces)))
        gain = gain * jnp.repeat(heights, extent[position] // shards_of).reshape([-1 if axis == position else 1 for axis in range(len(extent))])
    return gain


def centred(own_key, dims, deviation, most, pieces=(), held_as=jnp.bfloat16):
    factor_of = shard_levels(own_key, dims, pieces, -0.22, 0.18) if pieces else 1.0
    result = jax.random.normal(own_key, dims, jnp.float32) * deviation * factor_of
    return jnp.minimum(jnp.maximum(result, -most), most).astype(held_as)


def setup_inputs(seed: int = 0) -> dict:
    streams_of = jax.random.split(jax.random.key(seed), 6)
    return {
        "hidden_states": draw_hidden_states(jax.random.fold_in(streams_of[5], 71), 0),
        "proj_weight": centred(streams_of[1], (D, DA), (2 * D) ** -0.5, 0.0625, ((0, 128),)),
        "bilinear": centred(streams_of[2], (DA, DA), (DA * DA) ** -0.5, 0.005859375, ((0, 128),)),
        "lengths": draw_lengths(jax.random.fold_in(streams_of[5], 71), 0),
        "labels": plant((jax.random.randint(streams_of[4], (PROMPTS, NPAIRS), 0, 2) < 1).astype(jnp.int32), jax.random.fold_in(streams_of[4], 1), 0, 1),
    }


EPSILON = 1e-06
HIGH = lax.Precision.HIGHEST

def rounded(values):
    return lax.optimization_barrier(values.astype(jnp.bfloat16)).astype(jnp.float32)

def attend(query_rows, key_rows, key_valid):
    queries = query_rows.reshape(ROWS, HEADS, HEAD_DIM)
    keys = key_rows.reshape(ROWS, HEADS, HEAD_DIM)
    scores = jnp.einsum('thd,shd->hts', queries, keys, precision=HIGH) * HEAD_DIM ** (-0.5)
    scores = jnp.where(key_valid[None, None, :], scores, -jnp.inf)
    shifted = jnp.exp(scores - lax.optimization_barrier(jnp.max(scores, axis=2, keepdims=True)))
    weights = shifted / lax.optimization_barrier(jnp.sum(shifted, axis=2, keepdims=True))
    mixed = jnp.einsum('hts,shd->thd', rounded(weights), keys, precision=HIGH)
    return (weights, mixed)

def reference(hidden_states, proj_weight, bilinear, lengths, labels):
    first = jnp.asarray(np.array([a for a in range(CANDS) for b in range(CANDS) if a != b], np.int32))
    second = jnp.asarray(np.array([b for a in range(CANDS) for b in range(CANDS) if a != b], np.int32))
    upper_i, upper_j = np.triu_indices(CANDS, 1)
    offdiag = 1.0 - jnp.eye(CANDS, dtype=jnp.float32)
    bil32 = bilinear.astype(jnp.float32)

    def one_prompt(carry, inputs):
        grad_proj, grad_bil = carry
        hidden, length, label = inputs
        flat = hidden.reshape(CANDS * ROWS, D)
        projected = rounded(jnp.dot(flat, proj_weight, preferred_element_type=jnp.float32)).reshape(CANDS, ROWS, DA)
        positions = jnp.arange(ROWS, dtype=jnp.int32)
        valid = positions[None, :] < length[:, None]
        length_f = length.astype(jnp.float32)

        def pooled_mean(left, right):
            weights, mixed = attend(projected[left], projected[right], valid[right])
            total = lax.optimization_barrier(jnp.sum(jnp.where(valid[left][:, None, None], mixed, 0.0), axis=0))
            return total.reshape(DA) / length_f[left]
        means = jax.vmap(pooled_mean)(first, second)
        radius = jnp.sqrt(lax.optimization_barrier(jnp.mean(means * means, axis=1)) + EPSILON)
        normed = means / radius[:, None]
        pooled = jnp.zeros((CANDS, CANDS, DA), jnp.float32).at[first, second].set(normed)
        toward = jnp.einsum('ab,jib->ija', bil32, pooled, precision=HIGH)
        logits = lax.optimization_barrier(jnp.sum(pooled * toward, axis=2))
        wins = label.astype(jnp.float32)
        target = jnp.zeros((CANDS, CANDS), jnp.float32).at[upper_i, upper_j].set(wins).at[upper_j, upper_i].set(1.0 - wins)
        sign = 2.0 * target - 1.0
        dlogit = -sign * jax.nn.sigmoid(-sign * logits) * offdiag
        backward_dir = jnp.einsum('ba,jib->ija', bil32, pooled, precision=HIGH)
        dpooled = dlogit[:, :, None] * toward + dlogit.T[:, :, None] * backward_dir
        bil_term = jnp.einsum('ij,ija,jib->ab', dlogit, pooled, pooled, precision=HIGH)
        dnormed = dpooled[first, second]

        def pair_back(left, right, mean_row, radius_one, dnorm):
            weights, unused = attend(projected[left], projected[right], valid[right])
            norm_row = mean_row / radius_one
            dmean = (dnorm - norm_row * jnp.mean(dnorm * norm_row)) / radius_one
            dmean_heads = dmean.reshape(HEADS, HEAD_DIM)
            row_weight = jnp.where(valid[left], 1.0, 0.0) / length_f[left]
            keys = projected[right].reshape(ROWS, HEADS, HEAD_DIM)
            queries = projected[left].reshape(ROWS, HEADS, HEAD_DIM)
            along = jnp.einsum('shd,hd->hs', keys, dmean_heads, precision=HIGH)
            expected = jnp.einsum('hts,hs->ht', weights, along, precision=HIGH)
            dscore = row_weight[None, :, None] * weights * (along[:, None, :] - expected[:, :, None]) * HEAD_DIM ** (-0.5)
            dscore = rounded(dscore)
            dquery = jnp.einsum('hts,shd->thd', dscore, keys, precision=HIGH).reshape(ROWS, DA)
            column = jnp.einsum('hts,t->hs', weights, row_weight, precision=HIGH)
            dkey = jnp.einsum('hts,thd->shd', dscore, queries, precision=HIGH) + jnp.einsum('hs,hd->shd', column, dmean_heads, precision=HIGH)
            return (dquery, dkey.reshape(ROWS, DA))
        dqueries, dkeys = jax.vmap(pair_back)(first, second, means, radius, dnormed)
        drows = jnp.zeros((CANDS, ROWS, DA), jnp.float32).at[first].add(dqueries).at[second].add(dkeys)
        drows_b = drows.astype(jnp.bfloat16).reshape(CANDS * ROWS, DA)
        proj_term = jnp.dot(flat.T, drows_b, preferred_element_type=jnp.float32)
        return ((grad_proj + proj_term, grad_bil + bil_term), logits)
    start = (jnp.zeros((D, DA), jnp.float32), jnp.zeros((DA, DA), jnp.float32))
    (grad_proj, grad_bil), pair_logits = lax.scan(one_prompt, start, (hidden_states, lengths, labels))
    return (pair_logits, grad_proj, grad_bil)
```

```python
import jax
import jax.numpy as jnp
import numpy as np
from jax import lax
from jax.experimental import pallas as pl
from jax.experimental.pallas import tpu as pltpu
from jax.sharding import Mesh
from jax.sharding import PartitionSpec as P

HEAD_DIM = 64
CANDS = 8
ROWS = 128
SLICE = 128
WIDTH = 1024
PAIRS = CANDS * CANDS
EPSILON = 1e-06
FAR = 1e30
HIGH = lax.Precision.HIGHEST
BF = jnp.bfloat16
F32 = jnp.float32
NT = (((1,), (1,)), ((), ()))
NN = (((1,), (0,)), ((), ()))
TN = (((0,), (0,)), ((), ()))
CAND = ("xh", "z")
PROMPT = ("xl", "y", "core")


def mm(left, right, dims=NN, precision=None):
    return lax.dot_general(left, right, dims, precision=precision, preferred_element_type=F32)


def split(value):
    high = value.astype(BF)
    return high, (value - high.astype(F32)).astype(BF)


def lanes(shape):
    return lax.broadcasted_iota(jnp.int32, shape, len(shape) - 1)


def sublanes(shape):
    return lax.broadcasted_iota(jnp.int32, shape, len(shape) - 2)


def project_kernel(h_ref, w_ref, out_ref):
    depth = w_ref.shape[0] * w_ref.shape[2]
    h = h_ref[...].reshape(h_ref.shape[0] * ROWS, h_ref.shape[2])
    total = mm(h[:, :depth], w_ref[:, 0].reshape(depth, -1))
    total += mm(h[:, depth:], w_ref[:, 1].reshape(depth, -1))
    for dest in range(out_ref.shape[0]):
        out_ref[dest] = total[:, dest * SLICE : (dest + 1) * SLICE]


def project(h, w):
    steps = 4
    per = CANDS // steps
    dests = w.shape[3] // SLICE
    return pl.pallas_call(
        project_kernel,
        out_shape=jax.ShapeDtypeStruct((dests, CANDS * ROWS, SLICE), F32),
        grid=(steps,),
        in_specs=[
            pl.BlockSpec((per, ROWS, h.shape[2]), lambda s: (s, 0, 0)),
            pl.BlockSpec(w.shape, lambda s: (0, 0, 0, 0)),
        ],
        out_specs=pl.BlockSpec((dests, per * ROWS, SLICE), lambda s: (0, s, 0)),
        compiler_params=pltpu.CompilerParams(vmem_limit_bytes=24 << 20),
    )(h, w)


def head_queries(x_ref, i):
    rows = x_ref[pl.ds(pl.multiple_of(i * ROWS, ROWS), ROWS), :]
    lane = lanes(rows.shape)
    zero = jnp.zeros_like(rows)
    return jnp.concatenate(
        [jnp.where(lane < HEAD_DIM, rows, zero), jnp.where(lane < HEAD_DIM, zero, rows)], axis=0
    )


def forward_kernel(len_ref, p_ref, x_ref, mean_ref, col_ref, stat_ref, e_scr, m_scr, l_scr):
    total = p_ref[0]
    for source in range(1, p_ref.shape[0]):
        total += p_ref[source]
    x_ref[...] = total.astype(BF)
    wide = 2 * ROWS

    def one(i, carry):
        queries = head_queries(x_ref, i) * jnp.asarray(HEAD_DIM**-0.5, BF)
        own = len_ref[i]
        for j in range(CANDS):
            s = mm(x_ref[j * ROWS : (j + 1) * ROWS, :], queries, NT)
            s = jnp.where(sublanes(s.shape) < len_ref[j], s, -jnp.inf)
            m = jnp.max(s, axis=0, keepdims=True)
            e = jnp.exp(s - m)
            e_scr[j * ROWS : (j + 1) * ROWS, :] = e.astype(BF)
            m_scr[j : j + 1, :] = m
            l_scr[j : j + 1, :] = jnp.sum(e, axis=0, keepdims=True)
        shape = (CANDS, wide)
        token = jnp.bitwise_and(lanes(shape), ROWS - 1)
        live = jnp.logical_and(token < own, sublanes(shape) != i)
        weight = 1.0 / own.astype(F32)
        denom = l_scr[...]
        stat_ref[pl.ds(pl.multiple_of(i * CANDS, CANDS), CANDS), :] = jnp.where(
            live, m_scr[...] + jnp.log(denom) - jnp.log(weight * HEAD_DIM**-0.5), FAR
        )
        r = jnp.where(live, weight / denom, 0.0)
        first = lanes(shape) < ROWS
        r0h, r0l = split(jnp.where(first, r, 0.0))
        r1h, r1l = split(jnp.where(first, 0.0, r))
        got = mm(jnp.concatenate([r0h, r0l, r1h, r1l], axis=0), e_scr[...], NT)
        block = lanes((CANDS, CANDS * ROWS)) // ROWS == sublanes((CANDS, CANDS * ROWS))
        c0 = jnp.where(block, got[0:8] + got[8:16], 0.0)
        c1 = jnp.where(block, got[16:24] + got[24:32], 0.0)
        col_ref[i, 0:1, :] = jnp.sum(c0, axis=0, keepdims=True)
        col_ref[i, 1:2, :] = jnp.sum(c1, axis=0, keepdims=True)
        c0h, c0l = split(c0)
        c1h, c1l = split(c1)
        means = mm(jnp.concatenate([c0h, c0l, c1h, c1l], axis=0), x_ref[...])
        means = jnp.where(
            lanes((CANDS, SLICE)) < HEAD_DIM, means[0:8] + means[8:16], means[16:24] + means[24:32]
        )
        for dest in range(CANDS):
            mean_ref[dest, pl.ds(pl.multiple_of(i * CANDS, CANDS), CANDS), :] = means
        return carry

    lax.fori_loop(0, CANDS, one, 0)


def forward(lengths, parts):
    rows = CANDS * ROWS
    vmem = pl.BlockSpec(memory_space=pltpu.VMEM)
    return pl.pallas_call(
        forward_kernel,
        out_shape=(
            jax.ShapeDtypeStruct((rows, SLICE), BF),
            jax.ShapeDtypeStruct((CANDS, PAIRS, SLICE), F32),
            jax.ShapeDtypeStruct((CANDS, 2, rows), F32),
            jax.ShapeDtypeStruct((PAIRS, 2 * ROWS), F32),
        ),
        in_specs=[pl.BlockSpec(memory_space=pltpu.SMEM), vmem],
        out_specs=(vmem,) * 4,
        scratch_shapes=[
            pltpu.VMEM((rows, 2 * ROWS), BF),
            pltpu.VMEM((CANDS, 2 * ROWS), F32),
            pltpu.VMEM((CANDS, 2 * ROWS), F32),
        ],
        compiler_params=pltpu.CompilerParams(vmem_limit_bytes=16 << 20),
    )(lengths, parts)


def backward_kernel(
    len_ref, place_ref, mean_ref, bil_ref, x_ref, col_ref, stat_ref, sign_ref,
    dr_ref, logit_ref, term_ref,
    d_scr, along_scr, grad_scr,
):
    xh, z = place_ref[0], place_ref[1]
    here = xh * (CANDS // 2) + z
    means = jnp.concatenate([mean_ref[c] for c in range(CANDS)], axis=1)
    radius = jnp.sqrt(jnp.mean(means * means, axis=1, keepdims=True) + EPSILON)
    pooled = means / radius
    row, lane = sublanes((PAIRS, PAIRS)), lanes((PAIRS, PAIRS))
    swap = jnp.where(
        jnp.logical_and(row // CANDS == lane % CANDS, row % CANDS == lane // CANDS), 1.0, 0.0
    )
    reverse = mm(swap, pooled, precision=HIGH)
    rev_high, rev_low = split(reverse)
    both = mm(jnp.concatenate([rev_high, rev_low], axis=0), bil_ref[...], NT)
    toward = both[:PAIRS] + both[PAIRS:]
    logit = jnp.sum(pooled * toward, axis=1, keepdims=True)
    index = sublanes((PAIRS, 1))
    off = index // CANDS != index % CANDS
    logit = jnp.where(off, logit, 0.0)
    sign = sign_ref[...]
    dlogit = jnp.where(off, -sign * jax.nn.sigmoid(-sign * logit), 0.0)
    pick = lanes((PAIRS, SLICE))
    swapped = mm(
        swap, jnp.where(pick == 0, dlogit, jnp.where(pick == 1, logit, 0.0)), precision=HIGH
    )
    dlogit_rev, logit_rev = swapped[:, 0:1], swapped[:, 1:2]
    spread = jnp.where(
        lanes((PAIRS, SLICE)) == sublanes((PAIRS, SLICE)) % CANDS, logit, 0.0
    )
    gather = jnp.where(
        sublanes((CANDS, PAIRS)) == lanes((CANDS, PAIRS)) // CANDS, 1.0, 0.0
    )
    logit_ref[...] = mm(gather, spread, precision=HIGH)
    columns = pl.ds(pl.multiple_of(here * SLICE, SLICE), SLICE)
    back = mm(jnp.concatenate([rev_high, rev_low], axis=0), bil_ref[:, columns])
    back = back[:PAIRS] + back[PAIRS:]
    own_pooled = mean_ref[here] / radius
    own_toward = jnp.zeros((PAIRS, SLICE), F32)
    for c in range(CANDS):
        own_toward += jnp.where(here == c, toward[:, c * SLICE : (c + 1) * SLICE], 0.0)
    dpooled = dlogit * own_toward + dlogit_rev * back
    inner = (dlogit * logit + dlogit_rev * logit_rev) * (1.0 / WIDTH)
    dmeans = (dpooled - own_pooled * inner) / radius
    half = WIDTH // 2
    low_rows = jnp.concatenate(
        [mean_ref[z] / radius, mean_ref[z + CANDS // 2] / radius], axis=1
    ) * dlogit
    rev_half = jnp.where(xh == 0, reverse[:, :half], reverse[:, half:])
    ah, al = split(low_rows)
    bh, bl = split(rev_half)
    term_ref[...] = mm(
        jnp.concatenate([ah, al, ah], axis=0), jnp.concatenate([bh, bh, bl], axis=0), TN
    )
    dmeans_rev = mm(swap, dmeans, precision=HIGH)
    lane8 = lanes((CANDS, SLICE))
    turned = jnp.concatenate(
        [jnp.concatenate([col_ref[i] for i in range(CANDS)], axis=0)], axis=0
    ).T
    for j in range(CANDS):
        x = x_ref[j * ROWS : (j + 1) * ROWS, :]
        of_j = dmeans_rev[j * CANDS : (j + 1) * CANDS]
        heads = jnp.concatenate(
            [jnp.where(lane8 < HEAD_DIM, of_j, 0.0), jnp.where(lane8 < HEAD_DIM, 0.0, of_j)], axis=0
        )
        hh, hl = split(heads)
        along = mm(
            jnp.concatenate([x, x], axis=1),
            jnp.concatenate(
                [jnp.concatenate([hh, hl], axis=1), jnp.concatenate([hh, hl], axis=1)], axis=0
            ),
            NT,
        )
        ah, al = split(along)
        along_scr[j * ROWS : (j + 1) * ROWS, :] = jnp.where(lanes(along.shape) < 2 * CANDS, ah, al)
        spread_heads = jnp.zeros((2 * CANDS, SLICE), F32)
        order = sublanes((2 * CANDS, CANDS * 2)), lanes((2 * CANDS, CANDS * 2))
        to_heads = jnp.where(
            jnp.logical_and(order[0] // 2 == order[1] % CANDS, order[0] % 2 == order[1] // CANDS),
            1.0,
            0.0,
        )
        spread_heads = mm(to_heads, heads, precision=HIGH)
        grad_scr[j * ROWS : (j + 1) * ROWS, :] = mm(
            turned[j * ROWS : (j + 1) * ROWS, :], spread_heads, precision=HIGH
        )
    x_turned = x_ref[...].T
    wide = 2 * ROWS

    def one(i, carry):
        heads = head_queries(x_ref, i)
        queries = heads * jnp.asarray(HEAD_DIM**-0.5, BF)
        scale = len_ref[i].astype(F32) * HEAD_DIM**0.5
        shape = (4 * CANDS, wide)
        which = jnp.bitwise_and(sublanes(shape), 2 * CANDS - 1)
        chosen = jnp.where(
            which == jnp.where(lanes(shape) < ROWS, i, i + CANDS), 1.0, 0.0
        ).astype(BF)
        stats = stat_ref[pl.ds(pl.multiple_of(i * CANDS, CANDS), CANDS), :]
        for j in range(CANDS):
            s = mm(x_ref[j * ROWS : (j + 1) * ROWS, :], queries, NT)
            s = jnp.where(sublanes(s.shape) < len_ref[j], s, -jnp.inf)
            p = jnp.exp(s - stats[j : j + 1, :])
            along = mm(along_scr[j * ROWS : (j + 1) * ROWS, :], chosen)
            expected = jnp.sum(p * along, axis=0, keepdims=True) * scale
            d_scr[j * ROWS : (j + 1) * ROWS, :] = (p * (along - expected)).astype(BF)
        grad_scr[...] += mm(d_scr[...], heads)
        query = mm(x_turned, d_scr[...])
        query = jnp.concatenate([query[:HEAD_DIM, :ROWS], query[HEAD_DIM:, ROWS:]], axis=0)
        rows = pl.ds(pl.multiple_of(i * ROWS, ROWS), ROWS)
        grad_scr[rows, :] += query.T
        return carry

    lax.fori_loop(0, CANDS, one, 0)
    drows = grad_scr[...].astype(BF)
    for dest in range(dr_ref.shape[0]):
        dr_ref[dest] = drows


def backward(lengths, place, means, bil, x, col, stat, sign):
    rows = CANDS * ROWS
    vmem = pl.BlockSpec(memory_space=pltpu.VMEM)
    smem = pl.BlockSpec(memory_space=pltpu.SMEM)
    return pl.pallas_call(
        backward_kernel,
        out_shape=(
            jax.ShapeDtypeStruct((CANDS // 2, rows, SLICE), BF),
            jax.ShapeDtypeStruct((CANDS, SLICE), F32),
            jax.ShapeDtypeStruct((2 * SLICE, WIDTH // 2), F32),
        ),
        in_specs=[smem, smem] + [vmem] * 6,
        out_specs=(vmem,) * 3,
        scratch_shapes=[
            pltpu.VMEM((rows, 2 * ROWS), BF),
            pltpu.VMEM((rows, 4 * CANDS), BF),
            pltpu.VMEM((rows, SLICE), F32),
        ],
        compiler_params=pltpu.CompilerParams(vmem_limit_bytes=24 << 20),
    )(lengths, place, means, bil, x, col, stat, sign)


def gradient_kernel(h_ref, d_ref, term_ref, out_ref):
    count, rows, depth = h_ref.shape
    blocks, _, width = out_ref.shape
    h = h_ref[...].reshape(count * rows, depth)
    d = jnp.concatenate([d_ref[q] for q in range(d_ref.shape[0])], axis=1)
    total = mm(h, d, TN).reshape(blocks, depth // blocks, width)
    out_ref[...] = jnp.concatenate([total, term_ref[...]], axis=1).astype(BF)


def gradient(h, d, term):
    count, _, depth = h.shape
    steps = 4
    dests = term.shape[0]
    width = d.shape[0] * d.shape[2]
    block = depth // dests + term.shape[1]
    return pl.pallas_call(
        gradient_kernel,
        out_shape=jax.ShapeDtypeStruct((dests, block, width), BF),
        grid=(steps,),
        in_specs=[
            pl.BlockSpec((count, ROWS, depth // steps), lambda s: (0, 0, s)),
            pl.BlockSpec(d.shape, lambda s: (0, 0, 0)),
            pl.BlockSpec((dests // steps,) + term.shape[1:], lambda s: (s, 0, 0)),
        ],
        out_specs=pl.BlockSpec((dests // steps, block, width), lambda s: (s, 0, 0)),
        compiler_params=pltpu.CompilerParams(vmem_limit_bytes=24 << 20),
    )(h, d, term)


def finish_kernel(got_ref, proj_ref, bil_ref):
    half = got_ref.shape[2]
    count = got_ref.shape[0] // 2
    for part in range(2):
        total = got_ref[part * count].astype(F32)
        for source in range(1, count):
            total += got_ref[part * count + source].astype(F32)
        columns = slice(part * half, (part + 1) * half)
        proj_ref[:, columns] = total[: proj_ref.shape[0]]
        bil_ref[:, columns] = total[proj_ref.shape[0] :]


def finish(got, rows, bil_rows):
    vmem = pl.BlockSpec(memory_space=pltpu.VMEM)
    width = 2 * got.shape[2]
    return pl.pallas_call(
        finish_kernel,
        out_shape=(
            jax.ShapeDtypeStruct((rows, width), F32),
            jax.ShapeDtypeStruct((bil_rows, width), F32),
        ),
        in_specs=[vmem],
        out_specs=(vmem, vmem),
        compiler_params=pltpu.CompilerParams(vmem_limit_bytes=16 << 20),
    )(got)


def pair_signs():
    table = np.zeros((PAIRS, CANDS * (CANDS - 1) // 2), np.float32)
    upper_i, upper_j = np.triu_indices(CANDS, 1)
    for k, (i, j) in enumerate(zip(upper_i, upper_j)):
        table[i * CANDS + j, k] = 1.0
        table[j * CANDS + i, k] = -1.0
    return table


def body(hidden_states, proj_weight, bilinear, lengths, labels):
    xh, z = lax.axis_index("xh"), lax.axis_index("z")
    quarter = CANDS // 2
    lengths = lengths[0]
    hidden = hidden_states[0, 0]
    depth = hidden.shape[1]
    w = proj_weight.reshape(-1, 2, WIDTH // 2)
    other = lax.ppermute(jnp.where(xh == 0, w[:, 1], w[:, 0]), "xh", [(0, 1), (1, 0)])
    w = jnp.stack([jnp.where(xh == 0, w[:, 0], other), jnp.where(xh == 0, other, w[:, 1])])
    w = lax.all_gather(w, PROMPT, axis=0)
    h = hidden.reshape(ROWS, 2, quarter, depth // CANDS).transpose(2, 0, 1, 3)
    h = h.reshape(quarter, ROWS, depth // quarter)
    bil = jnp.broadcast_to(bilinear[None], (quarter,) + bilinear.shape)
    h = jnp.concatenate([h, bil], axis=1)
    h = jnp.broadcast_to(h[None], (2,) + h.shape).reshape((CANDS,) + h.shape[1:])
    h = lax.all_to_all(h, CAND, 0, 0)
    bil = lax.all_gather(h[:, ROWS:], PROMPT, axis=0)
    bil = bil.transpose(1, 0, 2, 3).reshape(WIDTH, WIDTH)
    parts = lax.all_to_all(project(h, w), "z", 0, 0)
    x, means, col, stat = forward(lengths, parts)
    means = lax.all_to_all(means, CAND, 0, 0)
    sign = 2.0 * labels[0].astype(F32) - 1.0
    sign = jnp.sum(pair_signs() * sign[None, :], axis=1, keepdims=True)
    drows, logits, term = backward(lengths, jnp.stack([xh, z]), means, bil, x, col, stat, sign)
    drows = lax.all_to_all(drows, "z", 0, 0)
    term = term.reshape(-1, bilinear.shape[0], term.shape[1])
    sent = gradient(h, drows, term)
    got = lax.all_to_all(sent, ("xh",) + PROMPT, 0, 0)
    grad_proj, grad_bil = finish(got, proj_weight.shape[0], bilinear.shape[0])
    return logits[None, :, :CANDS], grad_proj, grad_bil


def solution(mesh):
    parts = Mesh(mesh.devices.reshape(2, 4, 2, 4, 2), ("xh", "z", "xl", "y", "core"))
    in_specs = (
        P(PROMPT, CAND, None, None),
        P(CAND + PROMPT, None),
        P(CAND + PROMPT, None),
        P(PROMPT, None),
        P(PROMPT, None),
    )
    out_specs = (P(PROMPT, None, None), P(CAND + PROMPT, None), P(CAND + PROMPT, None))
    return jax.shard_map(body, mesh=parts, in_specs=in_specs, out_specs=out_specs, check_vma=False)
```

```python
import jax
import jax.numpy as jnp
import numpy as np
from jax import lax
from jax.experimental import pallas as pl
from jax.experimental.pallas import tpu as pltpu
from jax.sharding import Mesh
from jax.sharding import PartitionSpec as P

HEAD_DIM = 64
CANDS = 8
ROWS = 128
SLICE = 128
WIDTH = 1024
PAIRS = CANDS * CANDS
EPSILON = 1e-06
FAR = 1e30
HIGH = lax.Precision.HIGHEST
BF = jnp.bfloat16
F32 = jnp.float32
NT = (((1,), (1,)), ((), ()))
NN = (((1,), (0,)), ((), ()))
TN = (((0,), (0,)), ((), ()))
CAND = ("xh", "z")
PROMPT = ("xl", "y", "core")


def mm(left, right, dims=NN, precision=None):
    return lax.dot_general(left, right, dims, precision=precision, preferred_element_type=F32)


def split(value):
    high = value.astype(BF)
    return high, (value - high.astype(F32)).astype(BF)


def lanes(shape):
    return lax.broadcasted_iota(jnp.int32, shape, len(shape) - 1)


def sublanes(shape):
    return lax.broadcasted_iota(jnp.int32, shape, len(shape) - 2)


def pack_kernel(low_ref, high_ref, bil_ref, out_ref):
    half = low_ref.shape[1]
    bil = bil_ref[...]
    for dest in range(out_ref.shape[0]):
        out_ref[dest, 0, :ROWS, :half] = low_ref[...]
        out_ref[dest, 0, :ROWS, half:] = high_ref[...]
        out_ref[dest, 0, ROWS:, :] = jnp.concatenate([bil, bil], axis=0)


def pack(hidden, bil):
    quarter = CANDS // 2
    half = hidden.shape[1] // CANDS
    rows = ROWS + 2 * bil.shape[0]
    return pl.pallas_call(
        pack_kernel,
        out_shape=jax.ShapeDtypeStruct((2, quarter, rows, 2 * half), BF),
        grid=(quarter,),
        in_specs=[
            pl.BlockSpec((ROWS, half), lambda q: (0, q)),
            pl.BlockSpec((ROWS, half), lambda q: (0, q + CANDS // 2)),
            pl.BlockSpec(bil.shape, lambda q: (0, 0)),
        ],
        out_specs=pl.BlockSpec((2, 1, rows, 2 * half), lambda q: (0, q, 0, 0)),
        compiler_params=pltpu.CompilerParams(vmem_limit_bytes=16 << 20),
    )(hidden, hidden, bil)


def project_kernel(place_ref, h_ref, *refs):
    pieces, out_ref, w_scr = refs[:-2], refs[-2], refs[-1]
    count = len(pieces)

    @pl.when(pl.program_id(0) == 0)
    def _():
        for k, piece in enumerate(pieces):
            w_scr[:, :, lax.rem(place_ref[2] + count - k, count)] = piece[...]

    h = h_ref[...].reshape(h_ref.shape[0] * ROWS, h_ref.shape[2])
    total = mm(h, w_scr[...].reshape(h.shape[1], -1))
    for dest in range(out_ref.shape[0]):
        out_ref[dest] = total[:, dest * SLICE : (dest + 1) * SLICE]


def project(place, h, pieces):
    steps = 4
    per = CANDS // steps
    shape = pieces[0].shape
    dests = shape[3] // SLICE
    return pl.pallas_call(
        project_kernel,
        out_shape=jax.ShapeDtypeStruct((dests, CANDS * ROWS, SLICE), F32),
        grid=(steps,),
        in_specs=[
            pl.BlockSpec(memory_space=pltpu.SMEM),
            pl.BlockSpec((per, ROWS, h.shape[2]), lambda s: (s, 0, 0)),
        ]
        + [pl.BlockSpec(shape, lambda s: (0, 0, 0, 0))] * len(pieces),
        out_specs=pl.BlockSpec((dests, per * ROWS, SLICE), lambda s: (0, s, 0)),
        scratch_shapes=[pltpu.VMEM(shape[:2] + (len(pieces),) + shape[2:], BF)],
        compiler_params=pltpu.CompilerParams(vmem_limit_bytes=24 << 20),
    )(place, h, *pieces)


def extend(x, len_ref):
    blocks = []
    for j in range(CANDS):
        shape = (ROWS, SLICE)
        lane = lanes(shape)
        member = jnp.logical_and(lane < 3 * CANDS, jnp.bitwise_and(lane, CANDS - 1) == j)
        dead = jnp.logical_and(lane == 3 * CANDS, sublanes(shape) >= len_ref[j])
        blocks.append(jnp.where(dead, -FAR, jnp.where(member, 1.0, 0.0)).astype(BF))
    return jnp.concatenate([x, jnp.concatenate(blocks, axis=0)], axis=1)


def head_weights(xt_ref, i, shift=None):
    columns = xt_ref[:, i * ROWS : (i + 1) * ROWS] * jnp.asarray(HEAD_DIM**-0.5, BF)
    zero = jnp.zeros((HEAD_DIM, ROWS), BF)
    top = jnp.concatenate([columns[:HEAD_DIM], zero], axis=1)
    bottom = jnp.concatenate([zero, columns[HEAD_DIM:]], axis=1)
    wide = 2 * ROWS
    if shift is None:
        parts = [jnp.zeros((3 * CANDS, wide), F32)]
    else:
        high = shift.astype(BF).astype(F32)
        rest = shift - high
        middle = rest.astype(BF).astype(F32)
        parts = [-high, -middle, middle - rest]
    parts.append(jnp.where(sublanes((CANDS, wide)) == 0, 1.0, 0.0))
    extra = jnp.concatenate(parts, axis=0).astype(BF)
    return jnp.concatenate([top, bottom, extra, jnp.zeros((SLICE - 4 * CANDS, wide), BF)], axis=0)


def forward_kernel(len_ref, p_ref, x_ref, xt_ref, mean_ref, col_ref, stat_ref, e_scr, m_scr, l_scr):
    total = p_ref[0]
    for source in range(1, p_ref.shape[0]):
        total += p_ref[source]
    total = total.astype(BF)
    x_ref[...] = extend(total, len_ref)
    xt_ref[...] = total.T
    wide = 2 * ROWS
    for i in range(CANDS):
        weights = head_weights(xt_ref, i)
        for j in range(CANDS):
            s = mm(x_ref[j * ROWS : (j + 1) * ROWS, :], weights)
            m = jnp.max(s, axis=0, keepdims=True)
            e = jnp.exp(s - m)
            e_scr[i, j * ROWS : (j + 1) * ROWS, :] = e.astype(BF)
            m_scr[i, j : j + 1, :] = m
            l_scr[i, j : j + 1, :] = jnp.sum(e, axis=0, keepdims=True)
    for i in range(CANDS):
        own = len_ref[i]
        shape = (CANDS, wide)
        token = jnp.bitwise_and(lanes(shape), ROWS - 1)
        live = jnp.logical_and(token < own, sublanes(shape) != i)
        weight = 1.0 / own.astype(F32)
        denom = l_scr[i]
        stat_ref[i * CANDS : (i + 1) * CANDS, :] = jnp.where(
            live, m_scr[i] + jnp.log(denom) - jnp.log(weight * HEAD_DIM**-0.5), FAR
        )
        r = jnp.where(live, weight / denom, 0.0)
        first = lanes(shape) < ROWS
        r0h, r0l = split(jnp.where(first, r, 0.0))
        r1h, r1l = split(jnp.where(first, 0.0, r))
        got = mm(jnp.concatenate([r0h, r0l, r1h, r1l], axis=0), e_scr[i], NT)
        block = lanes((CANDS, CANDS * ROWS)) // ROWS == sublanes((CANDS, CANDS * ROWS))
        c0 = jnp.where(block, got[0:8] + got[8:16], 0.0)
        c1 = jnp.where(block, got[16:24] + got[24:32], 0.0)
        col_ref[0, i : i + 1, :] = jnp.sum(c0, axis=0, keepdims=True)
        col_ref[1, i : i + 1, :] = jnp.sum(c1, axis=0, keepdims=True)
        c0h, c0l = split(c0)
        c1h, c1l = split(c1)
        means = mm(jnp.concatenate([c0h, c0l, c1h, c1l], axis=0), x_ref[:, :SLICE])
        means = jnp.where(
            lanes((CANDS, SLICE)) < HEAD_DIM, means[0:8] + means[8:16], means[16:24] + means[24:32]
        )
        for dest in range(CANDS):
            mean_ref[dest, i * CANDS : (i + 1) * CANDS, :] = means


def forward(lengths, parts):
    rows = CANDS * ROWS
    vmem = pl.BlockSpec(memory_space=pltpu.VMEM)
    return pl.pallas_call(
        forward_kernel,
        out_shape=(
            jax.ShapeDtypeStruct((rows, 2 * SLICE), BF),
            jax.ShapeDtypeStruct((SLICE, rows), BF),
            jax.ShapeDtypeStruct((CANDS, PAIRS, SLICE), F32),
            jax.ShapeDtypeStruct((2, CANDS, rows), F32),
            jax.ShapeDtypeStruct((PAIRS, 2 * ROWS), F32),
        ),
        in_specs=[pl.BlockSpec(memory_space=pltpu.SMEM), vmem],
        out_specs=(vmem,) * 5,
        scratch_shapes=[
            pltpu.VMEM((CANDS, rows, 2 * ROWS), BF),
            pltpu.VMEM((CANDS, CANDS, 2 * ROWS), F32),
            pltpu.VMEM((CANDS, CANDS, 2 * ROWS), F32),
        ],
        compiler_params=pltpu.CompilerParams(vmem_limit_bytes=24 << 20),
    )(lengths, parts)


def backward_kernel(
    len_ref, place_ref, mean_ref, bil0_ref, bil1_ref, bil2_ref, bil3_ref,
    x_ref, xt_ref, col_ref, stat_ref, sign_ref, label_ref,
    dr_ref, logit_ref, term_ref,
    d_scr, along_scr, grad_scr, bil_scr,
):
    xh, z, y = place_ref[0], place_ref[1], place_ref[2]
    pieces = (bil0_ref, bil1_ref, bil2_ref, bil3_ref)
    for k, piece in enumerate(pieces):
        for part in range(2):
            bil_scr[:, part, lax.rem(y + len(pieces) - k, len(pieces))] = piece[part]
    here = xh * (CANDS // 2) + z
    means = jnp.concatenate([mean_ref[c] for c in range(CANDS)], axis=1)
    radius = jnp.sqrt(jnp.mean(means * means, axis=1, keepdims=True) + EPSILON)
    pooled = means / radius
    row, lane = sublanes((PAIRS, PAIRS)), lanes((PAIRS, PAIRS))
    swap = jnp.where(
        jnp.logical_and(row // CANDS == lane % CANDS, row % CANDS == lane // CANDS), 1.0, 0.0
    )
    reverse = mm(swap, pooled, precision=HIGH)
    rev_high, rev_low = split(reverse)
    both = mm(jnp.concatenate([rev_high, rev_low], axis=0), bil_scr[...].reshape(WIDTH, WIDTH), NT)
    toward = both[:PAIRS] + both[PAIRS:]
    logit = jnp.sum(pooled * toward, axis=1, keepdims=True)
    index = sublanes((PAIRS, 1))
    off = index // CANDS != index % CANDS
    logit = jnp.where(off, logit, 0.0)
    sign = jnp.sum(sign_ref[...] * (2.0 * label_ref[...].astype(F32) - 1.0), axis=1, keepdims=True)
    dlogit = jnp.where(off, -sign * jax.nn.sigmoid(-sign * logit), 0.0)
    pick = lanes((PAIRS, SLICE))
    swapped = mm(
        swap, jnp.where(pick == 0, dlogit, jnp.where(pick == 1, logit, 0.0)), precision=HIGH
    )
    dlogit_rev, logit_rev = swapped[:, 0:1], swapped[:, 1:2]
    spread = jnp.where(
        lanes((PAIRS, CANDS)) == sublanes((PAIRS, CANDS)) % CANDS, logit, 0.0
    )
    gather = jnp.where(
        sublanes((CANDS, PAIRS)) == lanes((CANDS, PAIRS)) // CANDS, 1.0, 0.0
    )
    logit_ref[...] = mm(gather, spread, precision=HIGH)
    columns = pl.ds(pl.multiple_of(here * SLICE, SLICE), SLICE)
    back = mm(
        jnp.concatenate([rev_high, rev_low], axis=0),
        bil_scr[:, :, :, :, columns].reshape(WIDTH, SLICE),
    )
    back = back[:PAIRS] + back[PAIRS:]
    own_pooled = mean_ref[here] / radius
    own_toward = jnp.zeros((PAIRS, SLICE), F32)
    for c in range(CANDS):
        own_toward += jnp.where(here == c, toward[:, c * SLICE : (c + 1) * SLICE], 0.0)
    dpooled = dlogit * own_toward + dlogit_rev * back
    inner = (dlogit * logit + dlogit_rev * logit_rev) * (1.0 / WIDTH)
    dmeans = (dpooled - own_pooled * inner) / radius
    half = WIDTH // 2
    low_rows = jnp.concatenate(
        [mean_ref[z] / radius, mean_ref[z + CANDS // 2] / radius], axis=1
    ) * dlogit
    rev_half = jnp.where(xh == 0, reverse[:, :half], reverse[:, half:])
    ah, al = split(low_rows)
    bh, bl = split(rev_half)
    term_ref[...] = mm(
        jnp.concatenate([ah, al, ah], axis=0), jnp.concatenate([bh, bh, bl], axis=0), TN
    )
    dmeans_rev = mm(swap, dmeans, precision=HIGH)
    lane8 = lanes((CANDS, SLICE))
    col = col_ref[...].reshape(2 * CANDS, CANDS * ROWS)
    col_high = col.astype(BF).astype(F32)
    turned = jnp.concatenate([col_high, col - col_high, col_high], axis=0).T.astype(BF)
    for j in range(CANDS):
        rows = slice(j * ROWS, (j + 1) * ROWS)
        x = x_ref[rows, :SLICE]
        of_j = dmeans_rev[j * CANDS : (j + 1) * CANDS]
        heads = jnp.concatenate(
            [jnp.where(lane8 < HEAD_DIM, of_j, 0.0), jnp.where(lane8 < HEAD_DIM, 0.0, of_j)], axis=0
        )
        hh, hl = split(heads)
        along = mm(
            jnp.concatenate([x, x], axis=1),
            jnp.concatenate(
                [jnp.concatenate([hh, hl], axis=1), jnp.concatenate([hh, hl], axis=1)], axis=0
            ),
            NT,
        )
        ah, al = split(along)
        along_scr[rows, :] = jnp.where(lanes(along.shape) < 2 * CANDS, ah, al)
        grad_scr[rows, :] = mm(turned[rows, :], jnp.concatenate([hh, hh, hl], axis=0))
    wide = 2 * ROWS
    for i in range(CANDS):
        weights = head_weights(xt_ref, i, stat_ref[i * CANDS : (i + 1) * CANDS, :])
        scale = len_ref[i].astype(F32) * HEAD_DIM**0.5
        shape = (4 * CANDS, wide)
        which = jnp.bitwise_and(sublanes(shape), 2 * CANDS - 1)
        chosen = jnp.where(
            which == jnp.where(lanes(shape) < ROWS, i, i + CANDS), 1.0, 0.0
        ).astype(BF)
        for j in range(CANDS):
            rows = slice(j * ROWS, (j + 1) * ROWS)
            p = jnp.exp(mm(x_ref[rows, :], weights))
            along = mm(along_scr[rows, :], chosen)
            expected = jnp.sum(p * along, axis=0, keepdims=True) * scale
            d_scr[i, rows, :] = (p * (along - expected)).astype(BF)
        lane = lanes((ROWS, SLICE))
        own = x_ref[i * ROWS : (i + 1) * ROWS, :SLICE]
        zero = jnp.zeros_like(own)
        heads = jnp.concatenate(
            [jnp.where(lane < HEAD_DIM, own, zero), jnp.where(lane < HEAD_DIM, zero, own)], axis=0
        )
        grad_scr[...] += mm(d_scr[i], heads)
        query = mm(xt_ref[...], d_scr[i])
        query = jnp.concatenate([query[:HEAD_DIM, :ROWS], query[HEAD_DIM:, ROWS:]], axis=0)
        grad_scr[i * ROWS : (i + 1) * ROWS, :] += query.T
    drows = grad_scr[...].astype(BF)
    for dest in range(dr_ref.shape[0]):
        dr_ref[dest] = drows


def backward(lengths, place, means, bil, x, xt, col, stat, labels):
    rows = CANDS * ROWS
    vmem = pl.BlockSpec(memory_space=pltpu.VMEM)
    smem = pl.BlockSpec(memory_space=pltpu.SMEM)
    return pl.pallas_call(
        backward_kernel,
        out_shape=(
            jax.ShapeDtypeStruct((CANDS // 2, rows, SLICE), BF),
            jax.ShapeDtypeStruct((CANDS, CANDS), F32),
            jax.ShapeDtypeStruct((2 * SLICE, WIDTH // 2), F32),
        ),
        in_specs=[smem, smem] + [vmem] * (7 + len(bil)),
        out_specs=(vmem,) * 3,
        scratch_shapes=[
            pltpu.VMEM((CANDS, rows, 2 * ROWS), BF),
            pltpu.VMEM((rows, 4 * CANDS), BF),
            pltpu.VMEM((rows, SLICE), F32),
            pltpu.VMEM((CANDS, 2, len(bil)) + bil[0].shape[2:], BF),
        ],
        compiler_params=pltpu.CompilerParams(vmem_limit_bytes=32 << 20),
    )(lengths, place, means, *bil, x, xt, col, stat, pair_signs(), labels)


def gradient_kernel(place_ref, h_ref, d_ref, term_ref, mine_ref, other_ref, scr):
    count, rows, depth = h_ref.shape
    groups, block, width = mine_ref.shape
    h = h_ref[...].reshape(count * rows, depth)
    d = jnp.concatenate([d_ref[q] for q in range(d_ref.shape[0])], axis=1)
    total = mm(h, d, TN).reshape(2 * groups, -1, width)
    total = jnp.concatenate([total, term_ref[...]], axis=1)
    scr[...] = total.reshape(groups, 2, block, width)
    core = place_ref[3]
    mine_ref[...] = scr[:, core]
    other_ref[...] = scr[:, 1 - core].astype(BF)


def gradient(place, h, d, term):
    count, _, depth = h.shape
    steps = 4
    dests = term.shape[0] // 2
    width = d.shape[0] * d.shape[2]
    block = depth // dests // 2 + term.shape[1]
    groups = dests // steps
    out = pl.BlockSpec((groups, block, width), lambda s: (s, 0, 0))
    return pl.pallas_call(
        gradient_kernel,
        out_shape=(
            jax.ShapeDtypeStruct((dests, block, width), F32),
            jax.ShapeDtypeStruct((dests, block, width), BF),
        ),
        grid=(steps,),
        in_specs=[
            pl.BlockSpec(memory_space=pltpu.SMEM),
            pl.BlockSpec((count, ROWS, depth // steps), lambda s: (0, 0, s)),
            pl.BlockSpec(d.shape, lambda s: (0, 0, 0)),
            pl.BlockSpec((2 * groups,) + term.shape[1:], lambda s: (s, 0, 0)),
        ],
        out_specs=(out, out),
        scratch_shapes=[pltpu.VMEM((groups, 2, block, width), F32)],
        compiler_params=pltpu.CompilerParams(vmem_limit_bytes=24 << 20),
    )(place, h, d, term)


def finish_kernel(got_ref, proj_ref, bil_ref):
    half = got_ref.shape[2]
    count = got_ref.shape[0] // 2
    for part in range(2):
        total = got_ref[part * count].astype(F32)
        for source in range(1, count):
            total += got_ref[part * count + source].astype(F32)
        columns = slice(part * half, (part + 1) * half)
        proj_ref[:, columns] = total[: proj_ref.shape[0]]
        bil_ref[:, columns] = total[proj_ref.shape[0] :]


def finish(got, rows, bil_rows):
    vmem = pl.BlockSpec(memory_space=pltpu.VMEM)
    width = 2 * got.shape[2]
    return pl.pallas_call(
        finish_kernel,
        out_shape=(
            jax.ShapeDtypeStruct((rows, width), F32),
            jax.ShapeDtypeStruct((bil_rows, width), F32),
        ),
        in_specs=[vmem],
        out_specs=(vmem, vmem),
        compiler_params=pltpu.CompilerParams(vmem_limit_bytes=16 << 20),
    )(got)


def pair_signs():
    table = np.zeros((PAIRS, CANDS * (CANDS - 1) // 2), np.float32)
    upper_i, upper_j = np.triu_indices(CANDS, 1)
    for k, (i, j) in enumerate(zip(upper_i, upper_j)):
        table[i * CANDS + j, k] = 1.0
        table[j * CANDS + i, k] = -1.0
    return table


def both(value, axis, dim):
    other = lax.ppermute(value, axis, [(0, 1), (1, 0)])
    first = lax.axis_index(axis) == 0
    return jnp.stack(
        [jnp.where(first, value, other), jnp.where(first, other, value)], axis=dim
    )


def around(value, axis):
    count = lax.axis_size(axis)
    return [value] + [
        lax.ppermute(value, axis, [(i, (i + k) % count) for i in range(count)])
        for k in range(1, count)
    ]


def gather_x(w):
    xh, xl = lax.axis_index("xh"), lax.axis_index("xl")
    half = w.shape[1] // 2
    keep = jnp.where(xh == 0, w[:, :half], w[:, half:])
    away = jnp.where(xh == 0, w[:, half:], w[:, :half])
    far, across, near = (
        lax.ppermute(value, ("xh", "xl"), [(i, i ^ flip) for i in range(4)])
        for value, flip in ((away, 2), (away, 3), (keep, 1))
    )
    same = jnp.where(xl == 0, jnp.stack([keep, near]), jnp.stack([near, keep]))
    cross = jnp.where(xl == 0, jnp.stack([far, across]), jnp.stack([across, far]))
    return jnp.where(xh == 0, jnp.stack([same, cross]), jnp.stack([cross, same]))


def body(hidden_states, proj_weight, bilinear, lengths, labels):
    xh, z, y, core = (lax.axis_index(axis) for axis in ("xh", "z", "y", "core"))
    lengths = lengths[0]
    w = gather_x(proj_weight)
    h = pack(hidden_states[0, 0], bilinear)
    h, w = lax.optimization_barrier((h, w))
    w = both(w, "core", 2)
    w = around(w.reshape(w.shape[:2] + (-1, w.shape[-1])), "y")
    h = lax.all_to_all(h.reshape((CANDS,) + h.shape[2:]), CAND, 0, 0)
    bil = both(h[:, ROWS : ROWS + bilinear.shape[0]], "core", 1)
    bil = both(bil.reshape(CANDS, -1, WIDTH), "xl", 0)
    bil = around(bil, "y")
    place = jnp.stack([xh, z, y, core])
    parts = lax.all_to_all(project(place, h, w), "z", 0, 0)
    x, xt, means, col, stat = forward(lengths, parts)
    means = lax.all_to_all(means, CAND, 0, 0)
    drows, logits, term = backward(lengths, place, means, bil, x, xt, col, stat, labels)
    drows = lax.all_to_all(drows, "z", 0, 0)
    term = term.reshape(-1, bilinear.shape[0], term.shape[1])
    mine, other = gradient(place, h, drows, term)
    other = lax.ppermute(other, "core", [(0, 1), (1, 0)])
    sent = (mine + other.astype(F32)).astype(BF)
    got = lax.all_to_all(sent, ("xh", "xl", "y"), 0, 0)
    grad_proj, grad_bil = finish(got, proj_weight.shape[0], bilinear.shape[0])
    return logits[None], grad_proj, grad_bil


def solution(mesh):
    parts = Mesh(mesh.devices.reshape(2, 4, 2, 4, 2), ("xh", "z", "xl", "y", "core"))
    in_specs = (
        P(PROMPT, CAND, None, None),
        P(CAND + PROMPT, None),
        P(CAND + PROMPT, None),
        P(PROMPT, None),
        P(PROMPT, None),
    )
    out_specs = (P(PROMPT, None, None), P(CAND + PROMPT, None), P(CAND + PROMPT, None))
    return jax.shard_map(body, mesh=parts, in_specs=in_specs, out_specs=out_specs, check_vma=False)
```

```python
import jax
import jax.numpy as jnp
from jax import lax
from jax.experimental import pallas as pl
from jax.experimental.pallas import tpu as pltpu
from jax.sharding import Mesh
from jax.sharding import PartitionSpec as P

HEAD_DIM = 64
CANDS = 8
ROWS = 128
SLICE = 128
WIDTH = 1024
PAIRS = CANDS * CANDS
EPSILON = 1e-06
FAR = 1e30
SCALE = 64.0
HIGH = lax.Precision.HIGHEST
BF = jnp.bfloat16
F32 = jnp.float32
NT = (((1,), (1,)), ((), ()))
NN = (((1,), (0,)), ((), ()))
TN = (((0,), (0,)), ((), ()))
CAND = ("xh", "z")
PROMPT = ("xl", "y", "core")


def mm(left, right, dims=NN, precision=None):
    return lax.dot_general(left, right, dims, precision=precision, preferred_element_type=F32)


def split(value):
    high = value.astype(BF)
    return high, (value - high.astype(F32)).astype(BF)


def lanes(shape):
    return lax.broadcasted_iota(jnp.int32, shape, len(shape) - 1)


def sublanes(shape):
    return lax.broadcasted_iota(jnp.int32, shape, len(shape) - 2)


def pack_kernel(low_ref, high_ref, bil_ref, out_ref):
    half = low_ref.shape[1]
    bil = bil_ref[...]
    for dest in range(out_ref.shape[0]):
        out_ref[dest, 0, :ROWS, :half] = low_ref[...]
        out_ref[dest, 0, :ROWS, half:] = high_ref[...]
        out_ref[dest, 0, ROWS:, :] = jnp.concatenate([bil, bil], axis=0)


def pack(hidden, bil):
    quarter = CANDS // 2
    half = hidden.shape[1] // CANDS
    rows = ROWS + 2 * bil.shape[0]
    hidden = pltpu.with_memory_space_constraint(hidden, pltpu.HBM)
    bil = pltpu.with_memory_space_constraint(bil, pltpu.HBM)
    return pl.pallas_call(
        pack_kernel,
        out_shape=jax.ShapeDtypeStruct((2, quarter, rows, 2 * half), BF),
        grid=(quarter,),
        in_specs=[
            pl.BlockSpec((ROWS, half), lambda q: (0, q)),
            pl.BlockSpec((ROWS, half), lambda q: (0, q + CANDS // 2)),
            pl.BlockSpec(bil.shape, lambda q: (0, 0)),
        ],
        out_specs=pl.BlockSpec((2, 1, rows, 2 * half), lambda q: (0, q, 0, 0)),
        compiler_params=pltpu.CompilerParams(vmem_limit_bytes=16 << 20),
    )(hidden, hidden, bil)


def project_kernel(place_ref, h_ref, *refs):
    pieces, (out_ref, w_scr) = refs[:-2], refs[-2:]
    count = len(pieces)

    @pl.when(pl.program_id(0) == 0)
    def _():
        for k, piece in enumerate(pieces):
            w_scr[:, :, lax.rem(place_ref[2] + count - k, count)] = piece[...]

    h = h_ref[...].reshape(h_ref.shape[0] * ROWS, h_ref.shape[2])
    total = mm(h, w_scr[...].reshape(h.shape[1], -1))
    for dest in range(out_ref.shape[0]):
        out_ref[dest] = total[:, dest * SLICE : (dest + 1) * SLICE]


def project(place, h, pieces):
    steps = 4
    per = CANDS // steps
    shape = pieces[0].shape
    depth = h.shape[2]
    dests = shape[3] // SLICE
    return pl.pallas_call(
        project_kernel,
        out_shape=jax.ShapeDtypeStruct((dests, CANDS * ROWS, SLICE), F32),
        grid=(steps,),
        in_specs=[
            pl.BlockSpec(memory_space=pltpu.SMEM),
            pl.BlockSpec((per, ROWS, depth), lambda s: (s, 0, 0)),
        ]
        + [pl.BlockSpec(shape, lambda s: (0, 0, 0, 0))] * len(pieces),
        out_specs=pl.BlockSpec((dests, per * ROWS, SLICE), lambda s: (0, s, 0)),
        scratch_shapes=[pltpu.VMEM(shape[:2] + (len(pieces),) + shape[2:], BF)],
        compiler_params=pltpu.CompilerParams(vmem_limit_bytes=24 << 20),
    )(place, h, *pieces)


def extend(x, len_ref):
    blocks = []
    for j in range(CANDS):
        shape = (ROWS, SLICE)
        lane = lanes(shape)
        member = jnp.logical_and(lane < 3 * CANDS, jnp.bitwise_and(lane, CANDS - 1) == j)
        dead = jnp.logical_and(lane == 3 * CANDS, sublanes(shape) >= len_ref[j])
        blocks.append(jnp.where(dead, -FAR, jnp.where(member, 1.0, 0.0)).astype(BF))
    return jnp.concatenate([x, jnp.concatenate(blocks, axis=0)], axis=1)


def head_weights(xt_ref, i, shift=None):
    columns = xt_ref[:, i * ROWS : (i + 1) * ROWS] * jnp.asarray(HEAD_DIM**-0.5, BF)
    zero = jnp.zeros((HEAD_DIM, ROWS), BF)
    top = jnp.concatenate([columns[:HEAD_DIM], zero], axis=1)
    bottom = jnp.concatenate([zero, columns[HEAD_DIM:]], axis=1)
    wide = 2 * ROWS
    if shift is None:
        parts = [jnp.zeros((3 * CANDS, wide), F32)]
    else:
        high = shift.astype(BF).astype(F32)
        rest = shift - high
        middle = rest.astype(BF).astype(F32)
        parts = [-high, -middle, middle - rest]
    parts.append(jnp.where(sublanes((CANDS, wide)) == 0, 1.0, 0.0))
    extra = jnp.concatenate(parts, axis=0).astype(BF)
    return jnp.concatenate([top, bottom, extra, jnp.zeros((SLICE - 4 * CANDS, wide), BF)], axis=0)


def forward_kernel(
    len_ref, x_ref, xt_ref, mean_ref, col_ref, stat_ref, e_scr, m_scr, l_scr, key_scr
):
    x = x_ref[...]
    key_scr[...] = extend(x, len_ref)
    xt_ref[...] = x.T
    wide = 2 * ROWS
    for i in range(CANDS):
        weights = head_weights(xt_ref, i)
        for j in range(CANDS):
            s = mm(key_scr[j * ROWS : (j + 1) * ROWS, :], weights)
            m = jnp.max(s, axis=0, keepdims=True)
            e = jnp.exp(s - m)
            e_scr[i, j * ROWS : (j + 1) * ROWS, :] = e.astype(BF)
            m_scr[i, j : j + 1, :] = m
            l_scr[i, j : j + 1, :] = jnp.sum(e, axis=0, keepdims=True)
    for i in range(CANDS):
        own = len_ref[i]
        shape = (CANDS, wide)
        token = jnp.bitwise_and(lanes(shape), ROWS - 1)
        live = jnp.logical_and(token < own, sublanes(shape) != i)
        weight = 1.0 / own.astype(F32)
        denom = l_scr[i]
        stat_ref[i * CANDS : (i + 1) * CANDS, :] = jnp.where(
            live, m_scr[i] + jnp.log(denom) - jnp.log(weight * HEAD_DIM**-0.5), FAR
        )
        r = jnp.where(live, weight / denom, 0.0)
        first = lanes(shape) < ROWS
        r0h, r0l = split(jnp.where(first, r, 0.0))
        r1h, r1l = split(jnp.where(first, 0.0, r))
        got = mm(jnp.concatenate([r0h, r0l, r1h, r1l], axis=0), e_scr[i], NT)
        block = lanes((CANDS, CANDS * ROWS)) // ROWS == sublanes((CANDS, CANDS * ROWS))
        c0 = jnp.where(block, got[0:8] + got[8:16], 0.0)
        c1 = jnp.where(block, got[16:24] + got[24:32], 0.0)
        col_ref[0, i : i + 1, :] = jnp.sum(c0, axis=0, keepdims=True)
        col_ref[1, i : i + 1, :] = jnp.sum(c1, axis=0, keepdims=True)
        c0h, c0l = split(c0)
        c1h, c1l = split(c1)
        means = mm(jnp.concatenate([c0h, c0l, c1h, c1l], axis=0), x_ref[...])
        means = jnp.where(
            lanes((CANDS, SLICE)) < HEAD_DIM, means[0:8] + means[8:16], means[16:24] + means[24:32]
        )
        for dest in range(CANDS):
            mean_ref[dest, i * CANDS : (i + 1) * CANDS, :] = means


def forward(lengths, x):
    rows = CANDS * ROWS
    vmem = pl.BlockSpec(memory_space=pltpu.VMEM)
    return pl.pallas_call(
        forward_kernel,
        out_shape=(
            jax.ShapeDtypeStruct((SLICE, rows), BF),
            jax.ShapeDtypeStruct((CANDS, PAIRS, SLICE), F32),
            jax.ShapeDtypeStruct((2, CANDS, rows), F32),
            jax.ShapeDtypeStruct((PAIRS, 2 * ROWS), F32),
        ),
        in_specs=[pl.BlockSpec(memory_space=pltpu.SMEM), vmem],
        out_specs=(vmem,) * 4,
        scratch_shapes=[
            pltpu.VMEM((CANDS, rows, 2 * ROWS), BF),
            pltpu.VMEM((CANDS, CANDS, 2 * ROWS), F32),
            pltpu.VMEM((CANDS, CANDS, 2 * ROWS), F32),
            pltpu.VMEM((rows, 2 * SLICE), BF),
        ],
        cost_estimate=pl.CostEstimate(flops=12 << 30, bytes_accessed=16 << 20, transcendentals=2 << 20),
        compiler_params=pltpu.CompilerParams(vmem_limit_bytes=24 << 20),
    )(lengths, x)


def backward_kernel(len_ref, place_ref, mean_ref, x_ref, xt_ref, col_ref, stat_ref, label_ref, *refs):
    bil_refs, refs = refs[:CANDS], refs[CANDS:]
    dr_ref, logit_ref, term_ref, d_scr, along_scr, grad_scr, key_scr, bil_scr = refs
    xh, z, y, core = place_ref[0], place_ref[1], place_ref[2], place_ref[3]
    count, half = len(bil_refs) // 2, WIDTH // 2
    for k in range(count):
        for piece, side in ((bil_refs[k], core), (bil_refs[count + k], 1 - core)):
            columns = pl.ds(pl.multiple_of(side * half, half), half)
            for part in range(2):
                bil_scr[:, part, lax.rem(y + count - k, count), :, columns] = piece[part]
    key_scr[...] = extend(x_ref[...], len_ref)
    here = xh * (CANDS // 2) + z
    means = jnp.concatenate([mean_ref[c] for c in range(CANDS)], axis=1)
    radius = jnp.sqrt(jnp.mean(means * means, axis=1, keepdims=True) + EPSILON)
    pooled = means / radius
    row, lane = sublanes((PAIRS, PAIRS)), lanes((PAIRS, PAIRS))
    swap = jnp.where(
        jnp.logical_and(row // CANDS == lane % CANDS, row % CANDS == lane // CANDS), 1.0, 0.0
    )
    reverse = mm(swap, pooled, precision=HIGH)
    rev_high, rev_low = split(reverse)
    both = mm(jnp.concatenate([rev_high, rev_low], axis=0), bil_scr[...].reshape(WIDTH, WIDTH), NT)
    toward = both[:PAIRS] + both[PAIRS:]
    logit = jnp.sum(pooled * toward, axis=1, keepdims=True)
    index = sublanes((PAIRS, 1))
    off = index // CANDS != index % CANDS
    logit = jnp.where(off, logit, 0.0)
    labels = label_ref[...]
    shape = (PAIRS, labels.shape[1])
    left, right = sublanes(shape) // CANDS, sublanes(shape) % CANDS
    low, high = jnp.minimum(left, right), jnp.maximum(left, right)
    spot = low * (2 * CANDS - 1 - low) // 2 + high - low - 1
    wins = (2.0 * labels.astype(F32) - 1.0) * jnp.where(left < right, 1.0, -1.0)
    sign = jnp.sum(jnp.where(spot == lanes(shape), wins, 0.0), axis=1, keepdims=True)
    dlogit = jnp.where(off, -sign * jax.nn.sigmoid(-sign * logit), 0.0)
    pick = lanes((PAIRS, SLICE))
    swapped = mm(
        swap, jnp.where(pick == 0, dlogit, jnp.where(pick == 1, logit, 0.0)), precision=HIGH
    )
    dlogit_rev, logit_rev = swapped[:, 0:1], swapped[:, 1:2]
    spread = jnp.where(
        lanes((PAIRS, CANDS)) == sublanes((PAIRS, CANDS)) % CANDS, logit, 0.0
    )
    gather = jnp.where(
        sublanes((CANDS, PAIRS)) == lanes((CANDS, PAIRS)) // CANDS, 1.0, 0.0
    )
    logit_ref[...] = mm(gather, spread, precision=HIGH)
    columns = pl.ds(pl.multiple_of(here * SLICE, SLICE), SLICE)
    back = mm(
        jnp.concatenate([rev_high, rev_low], axis=0),
        bil_scr[:, :, :, :, columns].reshape(WIDTH, SLICE),
    )
    back = back[:PAIRS] + back[PAIRS:]
    own_pooled = mean_ref[here] / radius
    own_toward = jnp.zeros((PAIRS, SLICE), F32)
    for c in range(CANDS):
        own_toward += jnp.where(here == c, toward[:, c * SLICE : (c + 1) * SLICE], 0.0)
    dpooled = dlogit * own_toward + dlogit_rev * back
    inner = (dlogit * logit + dlogit_rev * logit_rev) * (1.0 / WIDTH)
    dmeans = (dpooled - own_pooled * inner) / radius
    low_rows = jnp.concatenate(
        [mean_ref[z] / radius, mean_ref[z + CANDS // 2] / radius], axis=1
    ) * dlogit
    rev_half = jnp.where(xh == 0, reverse[:, :half], reverse[:, half:])
    ah, al = split(low_rows)
    bh, bl = split(rev_half)
    term_ref[...] = mm(
        jnp.concatenate([ah, al, ah], axis=0), jnp.concatenate([bh, bh, bl], axis=0), TN
    )
    dmeans_rev = mm(swap, dmeans, precision=HIGH)
    lane8 = lanes((CANDS, SLICE))
    col = col_ref[...].reshape(2 * CANDS, CANDS * ROWS)
    col_high = col.astype(BF).astype(F32)
    turned = jnp.concatenate([col_high, col - col_high, col_high], axis=0).T.astype(BF)
    for j in range(CANDS):
        rows = slice(j * ROWS, (j + 1) * ROWS)
        x = x_ref[rows, :]
        of_j = dmeans_rev[j * CANDS : (j + 1) * CANDS]
        heads = jnp.concatenate(
            [jnp.where(lane8 < HEAD_DIM, of_j, 0.0), jnp.where(lane8 < HEAD_DIM, 0.0, of_j)], axis=0
        )
        hh, hl = split(heads)
        along = mm(
            jnp.concatenate([x, x], axis=1),
            jnp.concatenate(
                [jnp.concatenate([hh, hl], axis=1), jnp.concatenate([hh, hl], axis=1)], axis=0
            ),
            NT,
        )
        ah, al = split(along)
        along_scr[rows, :] = jnp.where(lanes(along.shape) < 2 * CANDS, ah, al)
        grad_scr[rows, :] = mm(turned[rows, :], jnp.concatenate([hh, hh, hl], axis=0))
    wide = 2 * ROWS
    for i in range(CANDS):
        weights = head_weights(xt_ref, i, stat_ref[i * CANDS : (i + 1) * CANDS, :])
        scale = len_ref[i].astype(F32) * HEAD_DIM**0.5
        shape = (4 * CANDS, wide)
        which = jnp.bitwise_and(sublanes(shape), 2 * CANDS - 1)
        chosen = jnp.where(
            which == jnp.where(lanes(shape) < ROWS, i, i + CANDS), 1.0, 0.0
        ).astype(BF)
        for j in range(CANDS):
            rows = slice(j * ROWS, (j + 1) * ROWS)
            p = jnp.exp(mm(key_scr[rows, :], weights))
            along = mm(along_scr[rows, :], chosen)
            expected = jnp.sum(p * along, axis=0, keepdims=True) * scale
            d_scr[i, rows, :] = (p * (along - expected)).astype(BF)
        lane = lanes((ROWS, SLICE))
        own = x_ref[i * ROWS : (i + 1) * ROWS, :]
        zero = jnp.zeros_like(own)
        heads = jnp.concatenate(
            [jnp.where(lane < HEAD_DIM, own, zero), jnp.where(lane < HEAD_DIM, zero, own)], axis=0
        )
        grad_scr[...] += mm(d_scr[i], heads)
        query = mm(xt_ref[...], d_scr[i])
        query = jnp.concatenate([query[:HEAD_DIM, :ROWS], query[HEAD_DIM:, ROWS:]], axis=0)
        grad_scr[i * ROWS : (i + 1) * ROWS, :] += query.T
    drows = grad_scr[...].astype(BF)
    for dest in range(dr_ref.shape[0]):
        dr_ref[dest] = drows


def backward(lengths, place, means, bil, x, xt, col, stat, labels):
    rows = CANDS * ROWS
    vmem = pl.BlockSpec(memory_space=pltpu.VMEM)
    smem = pl.BlockSpec(memory_space=pltpu.SMEM)
    return pl.pallas_call(
        backward_kernel,
        out_shape=(
            jax.ShapeDtypeStruct((CANDS // 2, rows, SLICE), BF),
            jax.ShapeDtypeStruct((CANDS, CANDS), F32),
            jax.ShapeDtypeStruct((2 * SLICE, WIDTH // 2), F32),
        ),
        in_specs=[smem, smem] + [vmem] * (6 + len(bil)),
        out_specs=(vmem,) * 3,
        scratch_shapes=[
            pltpu.VMEM((CANDS, rows, 2 * ROWS), BF),
            pltpu.VMEM((rows, 4 * CANDS), BF),
            pltpu.VMEM((rows, SLICE), F32),
            pltpu.VMEM((rows, 2 * SLICE), BF),
            pltpu.VMEM((CANDS, 2, len(bil) // 2, 2 * CANDS, WIDTH), BF),
        ],
        compiler_params=pltpu.CompilerParams(vmem_limit_bytes=32 << 20),
    )(lengths, place, means, x, xt, col, stat, labels, *bil)


def gradient_kernel(place_ref, h_ref, d_ref, term_ref, mine_ref, other_ref, scr):
    count, rows, depth = h_ref.shape
    groups, block, width = mine_ref.shape
    h = h_ref[...].reshape(count * rows, depth)
    d = jnp.concatenate([d_ref[q] for q in range(d_ref.shape[0])], axis=1)
    total = mm(h, d, TN).reshape(2 * groups, -1, width)
    total = jnp.concatenate([total, term_ref[...]], axis=1)
    scr[...] = total.reshape(groups, 2, block, width)
    core = place_ref[3]
    mine_ref[...] = scr[:, core]
    other_ref[...] = scr[:, 1 - core].astype(BF)


def gradient(place, h, d, term):
    count, _, depth = h.shape
    steps = 4
    dests = term.shape[0] // 2
    width = d.shape[0] * d.shape[2]
    block = depth // dests // 2 + term.shape[1]
    groups = dests // steps
    out = pl.BlockSpec((groups, block, width), lambda s: (s, 0, 0))
    return pl.pallas_call(
        gradient_kernel,
        out_shape=(
            jax.ShapeDtypeStruct((dests, block, width), F32),
            jax.ShapeDtypeStruct((dests, block, width), BF),
        ),
        grid=(steps,),
        in_specs=[
            pl.BlockSpec(memory_space=pltpu.SMEM),
            pl.BlockSpec((count, ROWS, depth // steps), lambda s: (0, 0, s)),
            pl.BlockSpec(d.shape, lambda s: (0, 0, 0)),
            pl.BlockSpec((2 * groups,) + term.shape[1:], lambda s: (s, 0, 0)),
        ],
        out_specs=(out, out),
        scratch_shapes=[pltpu.VMEM((groups, 2, block, width), F32)],
        compiler_params=pltpu.CompilerParams(vmem_limit_bytes=24 << 20),
    )(place, h, d, term)


def finish_kernel(got_ref, proj_ref, bil_ref):
    half = got_ref.shape[2]
    count = got_ref.shape[0] // 2
    for part in range(2):
        total = got_ref[part * count].astype(F32)
        for source in range(1, count):
            total += got_ref[part * count + source].astype(F32)
        columns = slice(part * half, (part + 1) * half)
        proj_ref[:, columns] = total[: proj_ref.shape[0]]
        bil_ref[:, columns] = total[proj_ref.shape[0] :]


def finish(got, rows, bil_rows):
    vmem = pl.BlockSpec(memory_space=pltpu.VMEM)
    width = 2 * got.shape[2]
    return pl.pallas_call(
        finish_kernel,
        out_shape=(
            jax.ShapeDtypeStruct((rows, width), F32),
            jax.ShapeDtypeStruct((bil_rows, width), F32),
        ),
        in_specs=[vmem],
        out_specs=(vmem, vmem),
        compiler_params=pltpu.CompilerParams(vmem_limit_bytes=16 << 20),
    )(got)


def both(value, axis, dim):
    other = lax.ppermute(value, axis, [(0, 1), (1, 0)])
    first = lax.axis_index(axis) == 0
    return jnp.stack(
        [jnp.where(first, value, other), jnp.where(first, other, value)], axis=dim
    )


def around(value, axis):
    count = lax.axis_size(axis)
    return [value] + [
        lax.ppermute(value, axis, [(i, (i + k) % count) for i in range(count)])
        for k in range(1, count)
    ]


def gather_x(w):
    xh, xl = lax.axis_index("xh"), lax.axis_index("xl")
    half = w.shape[1] // 2
    keep = jnp.where(xh == 0, w[:, :half], w[:, half:])
    away = jnp.where(xh == 0, w[:, half:], w[:, :half])
    far, across, near = (
        lax.ppermute(value, ("xh", "xl"), [(i, i ^ flip) for i in range(4)])
        for value, flip in ((away, 2), (away, 3), (keep, 1))
    )
    same = jnp.where(xl == 0, jnp.stack([keep, near]), jnp.stack([near, keep]))
    cross = jnp.where(xl == 0, jnp.stack([far, across]), jnp.stack([across, far]))
    return jnp.where(xh == 0, jnp.stack([same, cross]), jnp.stack([cross, same]))


def gather_half(bil):
    core = lax.axis_index("core")
    half = bil.shape[2] // 2
    keep = jnp.where(core == 0, bil[:, :, :half], bil[:, :, half:])
    away = jnp.where(core == 0, bil[:, :, half:], bil[:, :, :half])
    other = lax.ppermute(away, "core", [(0, 1), (1, 0)])
    pair = [jnp.where(core == 0, keep, other), jnp.where(core == 0, other, keep)]
    return both(jnp.stack(pair, axis=1).reshape(bil.shape[0], -1, half), "xl", 0)


def body(hidden_states, proj_weight, bilinear, lengths, labels):
    xh, z, y, core = (lax.axis_index(axis) for axis in ("xh", "z", "y", "core"))
    place = jnp.stack([xh, z, y, core])
    lengths = lengths[0]
    w = gather_x(proj_weight)
    h = pack(hidden_states[0, 0], bilinear)
    h, w = lax.optimization_barrier((h, w))
    w = both(w, "core", 2)
    w = around(w.reshape(w.shape[:2] + (-1, w.shape[-1])), "y")
    h = lax.all_to_all(h.reshape((CANDS,) + h.shape[2:]), CAND, 0, 0)
    bil = around(gather_half(h[:, ROWS : ROWS + bilinear.shape[0]]), "y")
    parts = project(place, h, w)
    parts = lax.all_to_all((parts * SCALE).astype(jnp.float16), "z", 0, 0)
    x = (jnp.sum(parts.astype(F32), axis=0) * (1.0 / SCALE)).astype(BF)
    xt, means, col, stat = forward(lengths, x)
    bil, means = lax.optimization_barrier((bil, means))
    bil = bil + [lax.ppermute(piece, "core", [(0, 1), (1, 0)]) for piece in bil]
    means = lax.all_to_all(means, CAND, 0, 0)
    drows, logits, term = backward(lengths, place, means, bil, x, xt, col, stat, labels)
    drows = lax.all_to_all(drows, "z", 0, 0)
    term = term.reshape(-1, bilinear.shape[0], term.shape[1])
    mine, other = gradient(place, h, drows, term)
    other = lax.ppermute(other, "core", [(0, 1), (1, 0)])
    sent = (mine + other.astype(F32)).astype(BF)
    got = lax.all_to_all(sent, ("xh", "xl", "y"), 0, 0)
    grad_proj, grad_bil = finish(got, proj_weight.shape[0], bilinear.shape[0])
    return logits[None], grad_proj, grad_bil


def solution(mesh):
    parts = Mesh(mesh.devices.reshape(2, 4, 2, 4, 2), ("xh", "z", "xl", "y", "core"))
    in_specs = (
        P(PROMPT, CAND, None, None),
        P(CAND + PROMPT, None),
        P(CAND + PROMPT, None),
        P(PROMPT, None),
        P(PROMPT, None),
    )
    out_specs = (P(PROMPT, None, None), P(CAND + PROMPT, None), P(CAND + PROMPT, None))
    return jax.shard_map(body, mesh=parts, in_specs=in_specs, out_specs=out_specs, check_vma=False)
```

```python
import jax
import jax.numpy as jnp
from jax import lax
from jax.experimental import pallas as pl
from jax.experimental.pallas import tpu as pltpu
from jax.sharding import Mesh
from jax.sharding import PartitionSpec as P

HEAD_DIM = 64
CANDS = 8
ROWS = 128
SLICE = 128
WIDTH = 1024
PAIRS = CANDS * CANDS
EPSILON = 1e-06
FAR = 1e30
SCALE = 64.0
HIGH = lax.Precision.HIGHEST
BF = jnp.bfloat16
F32 = jnp.float32
NT = (((1,), (1,)), ((), ()))
NN = (((1,), (0,)), ((), ()))
TN = (((0,), (0,)), ((), ()))
CAND = ("xh", "z")
PROMPT = ("xl", "y", "core")


def mm(left, right, dims=NN, precision=None):
    return lax.dot_general(left, right, dims, precision=precision, preferred_element_type=F32)


def split(value):
    high = value.astype(BF)
    return high, (value - high.astype(F32)).astype(BF)


def lanes(shape):
    return lax.broadcasted_iota(jnp.int32, shape, len(shape) - 1)


def sublanes(shape):
    return lax.broadcasted_iota(jnp.int32, shape, len(shape) - 2)


def pack_kernel(low_ref, high_ref, out_ref):
    half = low_ref.shape[1]
    out_ref[0, :, :half] = low_ref[...]
    out_ref[0, :, half:] = high_ref[...]


def pack(hidden):
    quarter = CANDS // 2
    half = hidden.shape[1] // CANDS
    hidden = pltpu.with_memory_space_constraint(hidden, pltpu.HBM)
    return pl.pallas_call(
        pack_kernel,
        out_shape=jax.ShapeDtypeStruct((quarter, ROWS, 2 * half), BF),
        grid=(quarter,),
        in_specs=[
            pl.BlockSpec((ROWS, half), lambda q: (0, q)),
            pl.BlockSpec((ROWS, half), lambda q: (0, q + CANDS // 2)),
        ],
        out_specs=pl.BlockSpec((1, ROWS, 2 * half), lambda q: (q, 0, 0)),
        compiler_params=pltpu.CompilerParams(vmem_limit_bytes=16 << 20),
    )(hidden, hidden)


def project_kernel(place_ref, h_ref, *refs):
    pieces, (out_ref, w_scr) = refs[:-2], refs[-2:]
    count = len(pieces) // 2
    half = pieces[0].shape[3]

    @pl.when(pl.program_id(0) == 0)
    def _():
        for k in range(count):
            source = lax.rem(place_ref[2] + count - k, count)
            for piece, side in ((pieces[k], place_ref[3]), (pieces[count + k], 1 - place_ref[3])):
                columns = pl.ds(pl.multiple_of(side * half, half), half)
                w_scr[:, :, source, :, columns] = piece[...]

    h = h_ref[...].reshape(h_ref.shape[0] * ROWS, h_ref.shape[2])
    total = mm(h, w_scr[...].reshape(h.shape[1], -1))
    for dest in range(out_ref.shape[0]):
        out_ref[dest] = total[:, dest * SLICE : (dest + 1) * SLICE]


def project(place, h, pieces):
    steps = 2
    per = h.shape[0] // steps
    shape = pieces[0].shape
    depth = h.shape[2]
    count = len(pieces) // 2
    width = 2 * shape[3]
    dests = width // SLICE
    return pl.pallas_call(
        project_kernel,
        out_shape=jax.ShapeDtypeStruct((dests, h.shape[0] * ROWS, SLICE), F32),
        grid=(steps,),
        in_specs=[
            pl.BlockSpec(memory_space=pltpu.SMEM),
            pl.BlockSpec((per, ROWS, depth), lambda s: (s, 0, 0)),
        ]
        + [pl.BlockSpec(shape, lambda s: (0, 0, 0, 0))] * len(pieces),
        out_specs=pl.BlockSpec((dests, per * ROWS, SLICE), lambda s: (0, s, 0)),
        scratch_shapes=[pltpu.VMEM(shape[:2] + (count, shape[2], width), BF)],
        compiler_params=pltpu.CompilerParams(vmem_limit_bytes=32 << 20),
    )(place, h, *pieces)


def extend(x, len_ref):
    blocks = []
    for j in range(CANDS):
        shape = (ROWS, SLICE)
        lane = lanes(shape)
        member = jnp.logical_and(lane < 3 * CANDS, jnp.bitwise_and(lane, CANDS - 1) == j)
        dead = jnp.logical_and(lane == 3 * CANDS, sublanes(shape) >= len_ref[j])
        blocks.append(jnp.where(dead, -FAR, jnp.where(member, 1.0, 0.0)).astype(BF))
    return jnp.concatenate([x, jnp.concatenate(blocks, axis=0)], axis=1)


def head_weights(xt_ref, i, shift=None):
    columns = xt_ref[:, i * ROWS : (i + 1) * ROWS] * jnp.asarray(HEAD_DIM**-0.5, BF)
    zero = jnp.zeros((HEAD_DIM, ROWS), BF)
    top = jnp.concatenate([columns[:HEAD_DIM], zero], axis=1)
    bottom = jnp.concatenate([zero, columns[HEAD_DIM:]], axis=1)
    wide = 2 * ROWS
    if shift is None:
        parts = [jnp.zeros((3 * CANDS, wide), F32)]
    else:
        high = shift.astype(BF).astype(F32)
        rest = shift - high
        middle = rest.astype(BF).astype(F32)
        parts = [-high, -middle, middle - rest]
    parts.append(jnp.where(sublanes((CANDS, wide)) == 0, 1.0, 0.0))
    extra = jnp.concatenate(parts, axis=0).astype(BF)
    return jnp.concatenate([top, bottom, extra, jnp.zeros((SLICE - 4 * CANDS, wide), BF)], axis=0)


def forward_kernel(
    len_ref, x_ref, xt_ref, mean_ref, col_ref, stat_ref, e_scr, m_scr, l_scr, key_scr
):
    x = x_ref[...]
    key_scr[...] = extend(x, len_ref)
    xt_ref[...] = x.T
    wide = 2 * ROWS
    for i in range(CANDS):
        weights = head_weights(xt_ref, i)
        for j in range(CANDS):
            s = mm(key_scr[j * ROWS : (j + 1) * ROWS, :], weights)
            m = jnp.max(s, axis=0, keepdims=True)
            e = jnp.exp(s - m)
            e_scr[i, j * ROWS : (j + 1) * ROWS, :] = e.astype(BF)
            m_scr[i, j : j + 1, :] = m
            l_scr[i, j : j + 1, :] = jnp.sum(e, axis=0, keepdims=True)
    for i in range(CANDS):
        own = len_ref[i]
        shape = (CANDS, wide)
        token = jnp.bitwise_and(lanes(shape), ROWS - 1)
        live = jnp.logical_and(token < own, sublanes(shape) != i)
        weight = 1.0 / own.astype(F32)
        denom = l_scr[i]
        stat_ref[i * CANDS : (i + 1) * CANDS, :] = jnp.where(
            live, m_scr[i] + jnp.log(denom) - jnp.log(weight * HEAD_DIM**-0.5), FAR
        )
        r = jnp.where(live, weight / denom, 0.0)
        first = lanes(shape) < ROWS
        r0h, r0l = split(jnp.where(first, r, 0.0))
        r1h, r1l = split(jnp.where(first, 0.0, r))
        got = mm(jnp.concatenate([r0h, r0l, r1h, r1l], axis=0), e_scr[i], NT)
        block = lanes((CANDS, CANDS * ROWS)) // ROWS == sublanes((CANDS, CANDS * ROWS))
        c0 = jnp.where(block, got[0:8] + got[8:16], 0.0)
        c1 = jnp.where(block, got[16:24] + got[24:32], 0.0)
        col_ref[0, i : i + 1, :] = jnp.sum(c0, axis=0, keepdims=True)
        col_ref[1, i : i + 1, :] = jnp.sum(c1, axis=0, keepdims=True)
        c0h, c0l = split(c0)
        c1h, c1l = split(c1)
        means = mm(jnp.concatenate([c0h, c0l, c1h, c1l], axis=0), x_ref[...])
        means = jnp.where(
            lanes((CANDS, SLICE)) < HEAD_DIM, means[0:8] + means[8:16], means[16:24] + means[24:32]
        )
        for dest in range(CANDS):
            mean_ref[dest, i * CANDS : (i + 1) * CANDS, :] = means


def forward(lengths, x):
    rows = CANDS * ROWS
    vmem = pl.BlockSpec(memory_space=pltpu.VMEM)
    return pl.pallas_call(
        forward_kernel,
        out_shape=(
            jax.ShapeDtypeStruct((SLICE, rows), BF),
            jax.ShapeDtypeStruct((CANDS, PAIRS, SLICE), F32),
            jax.ShapeDtypeStruct((2, CANDS, rows), F32),
            jax.ShapeDtypeStruct((PAIRS, 2 * ROWS), F32),
        ),
        in_specs=[pl.BlockSpec(memory_space=pltpu.SMEM), vmem],
        out_specs=(vmem,) * 4,
        scratch_shapes=[
            pltpu.VMEM((CANDS, rows, 2 * ROWS), BF),
            pltpu.VMEM((CANDS, CANDS, 2 * ROWS), F32),
            pltpu.VMEM((CANDS, CANDS, 2 * ROWS), F32),
            pltpu.VMEM((rows, 2 * SLICE), BF),
        ],
        cost_estimate=pl.CostEstimate(flops=12 << 30, bytes_accessed=16 << 20, transcendentals=2 << 20),
        compiler_params=pltpu.CompilerParams(vmem_limit_bytes=24 << 20),
    )(lengths, x)


def backward_kernel(len_ref, place_ref, mean_ref, x_ref, xt_ref, col_ref, stat_ref, label_ref, *refs):
    bil_refs, refs = refs[:CANDS], refs[CANDS:]
    dr_ref, logit_ref, term_ref, d_scr, along_scr, grad_scr, key_scr, bil_scr = refs
    xh, z, y, core = place_ref[0], place_ref[1], place_ref[2], place_ref[3]
    count, half = len(bil_refs) // 2, WIDTH // 2
    for k in range(count):
        for piece, side in ((bil_refs[k], core), (bil_refs[count + k], 1 - core)):
            columns = pl.ds(pl.multiple_of(side * half, half), half)
            for hi, lo in ((0, 0), (0, 1), (1, 0), (1, 1)):
                for back in range(piece.shape[2]):
                    level = lax.rem(z + piece.shape[2] - back, piece.shape[2])
                    bil_scr[hi, level, lo, lax.rem(y + count - k, count), :, columns] = piece[hi, lo, back]
    key_scr[...] = extend(x_ref[...], len_ref)
    here = xh * (CANDS // 2) + z
    means = jnp.concatenate([mean_ref[c] for c in range(CANDS)], axis=1)
    radius = jnp.sqrt(jnp.mean(means * means, axis=1, keepdims=True) + EPSILON)
    pooled = means / radius
    row, lane = sublanes((PAIRS, PAIRS)), lanes((PAIRS, PAIRS))
    swap = jnp.where(
        jnp.logical_and(row // CANDS == lane % CANDS, row % CANDS == lane // CANDS), 1.0, 0.0
    )
    reverse = mm(swap, pooled, precision=HIGH)
    rev_high, rev_low = split(reverse)
    both = mm(jnp.concatenate([rev_high, rev_low], axis=0), bil_scr[...].reshape(WIDTH, WIDTH), NT)
    toward = both[:PAIRS] + both[PAIRS:]
    logit = jnp.sum(pooled * toward, axis=1, keepdims=True)
    index = sublanes((PAIRS, 1))
    off = index // CANDS != index % CANDS
    logit = jnp.where(off, logit, 0.0)
    labels = label_ref[...]
    shape = (PAIRS, labels.shape[1])
    left, right = sublanes(shape) // CANDS, sublanes(shape) % CANDS
    low, high = jnp.minimum(left, right), jnp.maximum(left, right)
    spot = low * (2 * CANDS - 1 - low) // 2 + high - low - 1
    wins = (2.0 * labels.astype(F32) - 1.0) * jnp.where(left < right, 1.0, -1.0)
    sign = jnp.sum(jnp.where(spot == lanes(shape), wins, 0.0), axis=1, keepdims=True)
    dlogit = jnp.where(off, -sign * jax.nn.sigmoid(-sign * logit), 0.0)
    pick = lanes((PAIRS, SLICE))
    swapped = mm(
        swap, jnp.where(pick == 0, dlogit, jnp.where(pick == 1, logit, 0.0)), precision=HIGH
    )
    dlogit_rev, logit_rev = swapped[:, 0:1], swapped[:, 1:2]
    spread = jnp.where(
        lanes((PAIRS, CANDS)) == sublanes((PAIRS, CANDS)) % CANDS, logit, 0.0
    )
    gather = jnp.where(
        sublanes((CANDS, PAIRS)) == lanes((CANDS, PAIRS)) // CANDS, 1.0, 0.0
    )
    logit_ref[...] = mm(gather, spread, precision=HIGH)
    columns = pl.ds(pl.multiple_of(here * SLICE, SLICE), SLICE)
    back = mm(
        jnp.concatenate([rev_high, rev_low], axis=0),
        bil_scr[:, :, :, :, :, columns].reshape(WIDTH, SLICE),
    )
    back = back[:PAIRS] + back[PAIRS:]
    own_pooled = mean_ref[here] / radius
    own_toward = jnp.zeros((PAIRS, SLICE), F32)
    for c in range(CANDS):
        own_toward += jnp.where(here == c, toward[:, c * SLICE : (c + 1) * SLICE], 0.0)
    dpooled = dlogit * own_toward + dlogit_rev * back
    inner = (dlogit * logit + dlogit_rev * logit_rev) * (1.0 / WIDTH)
    dmeans = (dpooled - own_pooled * inner) / radius
    low_rows = jnp.concatenate(
        [mean_ref[z] / radius, mean_ref[z + CANDS // 2] / radius], axis=1
    ) * dlogit
    rev_half = jnp.where(xh == 0, reverse[:, :half], reverse[:, half:])
    ah, al = split(low_rows)
    bh, bl = split(rev_half)
    term_ref[...] = mm(
        jnp.concatenate([ah, al, ah], axis=0), jnp.concatenate([bh, bh, bl], axis=0), TN
    )
    dmeans_rev = mm(swap, dmeans, precision=HIGH)
    lane8 = lanes((CANDS, SLICE))
    col = col_ref[...].reshape(2 * CANDS, CANDS * ROWS)
    col_high = col.astype(BF).astype(F32)
    turned = jnp.concatenate([col_high, col - col_high, col_high], axis=0).T.astype(BF)
    for j in range(CANDS):
        rows = slice(j * ROWS, (j + 1) * ROWS)
        x = x_ref[rows, :]
        of_j = dmeans_rev[j * CANDS : (j + 1) * CANDS]
        heads = jnp.concatenate(
            [jnp.where(lane8 < HEAD_DIM, of_j, 0.0), jnp.where(lane8 < HEAD_DIM, 0.0, of_j)], axis=0
        )
        hh, hl = split(heads)
        along = mm(
            jnp.concatenate([x, x], axis=1),
            jnp.concatenate(
                [jnp.concatenate([hh, hl], axis=1), jnp.concatenate([hh, hl], axis=1)], axis=0
            ),
            NT,
        )
        ah, al = split(along)
        along_scr[rows, :] = jnp.where(lanes(along.shape) < 2 * CANDS, ah, al)
        grad_scr[rows, :] = mm(turned[rows, :], jnp.concatenate([hh, hh, hl], axis=0))
    wide = 2 * ROWS
    for i in range(CANDS):
        weights = head_weights(xt_ref, i, stat_ref[i * CANDS : (i + 1) * CANDS, :])
        scale = len_ref[i].astype(F32) * HEAD_DIM**0.5
        shape = (4 * CANDS, wide)
        which = jnp.bitwise_and(sublanes(shape), 2 * CANDS - 1)
        chosen = jnp.where(
            which == jnp.where(lanes(shape) < ROWS, i, i + CANDS), 1.0, 0.0
        ).astype(BF)
        for j in range(CANDS):
            rows = slice(j * ROWS, (j + 1) * ROWS)
            p = jnp.exp(mm(key_scr[rows, :], weights))
            along = mm(along_scr[rows, :], chosen)
            expected = jnp.sum(p * along, axis=0, keepdims=True) * scale
            d_scr[i, rows, :] = (p * (along - expected)).astype(BF)
        lane = lanes((ROWS, SLICE))
        own = x_ref[i * ROWS : (i + 1) * ROWS, :]
        zero = jnp.zeros_like(own)
        heads = jnp.concatenate(
            [jnp.where(lane < HEAD_DIM, own, zero), jnp.where(lane < HEAD_DIM, zero, own)], axis=0
        )
        grad_scr[...] += mm(d_scr[i], heads)
        query = mm(xt_ref[...], d_scr[i])
        query = jnp.concatenate([query[:HEAD_DIM, :ROWS], query[HEAD_DIM:, ROWS:]], axis=0)
        grad_scr[i * ROWS : (i + 1) * ROWS, :] += query.T
    drows = grad_scr[...].astype(BF)
    for dest in range(dr_ref.shape[0]):
        dr_ref[dest] = drows


def backward(lengths, place, means, bil, x, xt, col, stat, labels):
    rows = CANDS * ROWS
    vmem = pl.BlockSpec(memory_space=pltpu.VMEM)
    smem = pl.BlockSpec(memory_space=pltpu.SMEM)
    return pl.pallas_call(
        backward_kernel,
        out_shape=(
            jax.ShapeDtypeStruct((CANDS // 2, rows, SLICE), BF),
            jax.ShapeDtypeStruct((CANDS, CANDS), F32),
            jax.ShapeDtypeStruct((2 * SLICE, WIDTH // 2), F32),
        ),
        in_specs=[smem, smem] + [vmem] * (6 + len(bil)),
        out_specs=(vmem,) * 3,
        scratch_shapes=[
            pltpu.VMEM((CANDS, rows, 2 * ROWS), BF),
            pltpu.VMEM((rows, 4 * CANDS), BF),
            pltpu.VMEM((rows, SLICE), F32),
            pltpu.VMEM((rows, 2 * SLICE), BF),
            pltpu.VMEM((2, CANDS // 2, 2, len(bil) // 2, 2 * CANDS, WIDTH), BF),
        ],
        cost_estimate=pl.CostEstimate(flops=8 << 30, bytes_accessed=8 << 20, transcendentals=2 << 20),
        compiler_params=pltpu.CompilerParams(vmem_limit_bytes=32 << 20),
    )(lengths, place, means, x, xt, col, stat, labels, *bil)


def gradient_kernel(place_ref, h_ref, far_ref, d_ref, term_ref, mine_ref, other_ref, d_scr, scr):
    count, rows, depth = h_ref.shape
    groups, block, width = mine_ref.shape
    rows *= count

    @pl.when(pl.program_id(0) == 0)
    def _():
        for part, side in ((0, place_ref[0]), (1, 1 - place_ref[0])):
            source = pl.ds(pl.multiple_of(side * rows, rows), rows)
            for q in range(d_ref.shape[0]):
                d_scr[part * rows : (part + 1) * rows, q * SLICE : (q + 1) * SLICE] = d_ref[q, source, :]

    h = jnp.concatenate([h_ref[...].reshape(rows, depth), far_ref[...].reshape(rows, depth)], axis=0)
    total = mm(h, d_scr[...], TN).reshape(2 * groups, -1, width)
    total = jnp.concatenate([total, term_ref[...]], axis=1)
    scr[...] = total.reshape(groups, 2, block, width)
    core = place_ref[3]
    mine_ref[...] = scr[:, core]
    other_ref[...] = scr[:, 1 - core].astype(BF)


def gradient(place, h, far, d, term):
    count, _, depth = h.shape
    steps = 4
    dests = term.shape[0] // 2
    width = d.shape[0] * d.shape[2]
    block = depth // dests // 2 + term.shape[1]
    groups = dests // steps
    out = pl.BlockSpec((groups, block, width), lambda s: (s, 0, 0))
    hidden = pl.BlockSpec((count, ROWS, depth // steps), lambda s: (0, 0, s))
    return pl.pallas_call(
        gradient_kernel,
        out_shape=(
            jax.ShapeDtypeStruct((dests, block, width), F32),
            jax.ShapeDtypeStruct((dests, block, width), BF),
        ),
        grid=(steps,),
        in_specs=[
            pl.BlockSpec(memory_space=pltpu.SMEM),
            hidden,
            hidden,
            pl.BlockSpec(d.shape, lambda s: (0, 0, 0)),
            pl.BlockSpec((2 * groups,) + term.shape[1:], lambda s: (s, 0, 0)),
        ],
        out_specs=(out, out),
        scratch_shapes=[
            pltpu.VMEM((d.shape[1], width), BF),
            pltpu.VMEM((groups, 2, block, width), F32),
        ],
        compiler_params=pltpu.CompilerParams(vmem_limit_bytes=24 << 20),
    )(place, h, far, d, term)


def finish_kernel(got_ref, proj_ref, bil_ref):
    half = got_ref.shape[2]
    count = got_ref.shape[0] // 2
    for part in range(2):
        total = got_ref[part * count].astype(F32)
        for source in range(1, count):
            total += got_ref[part * count + source].astype(F32)
        columns = slice(part * half, (part + 1) * half)
        proj_ref[:, columns] = total[: proj_ref.shape[0]]
        bil_ref[:, columns] = total[proj_ref.shape[0] :]


def finish(got, rows, bil_rows):
    vmem = pl.BlockSpec(memory_space=pltpu.VMEM)
    width = 2 * got.shape[2]
    return pl.pallas_call(
        finish_kernel,
        out_shape=(
            jax.ShapeDtypeStruct((rows, width), F32),
            jax.ShapeDtypeStruct((bil_rows, width), F32),
        ),
        in_specs=[vmem],
        out_specs=(vmem, vmem),
        compiler_params=pltpu.CompilerParams(vmem_limit_bytes=16 << 20),
    )(got)


SWAP = [(0, 1), (1, 0)]


def gather_core(value):
    first = lax.axis_index("core") == 0
    half = value.shape[-1] // 2
    keep = jnp.where(first, value[..., :half], value[..., half:])
    away = jnp.where(first, value[..., half:], value[..., :half])
    other = lax.ppermute(away, "core", SWAP)
    return jnp.concatenate(
        [jnp.where(first, keep, other), jnp.where(first, other, keep)], axis=-2
    )


def gather_x(value):
    xh, xl = lax.axis_index("xh"), lax.axis_index("xl")
    far, across, near = (
        lax.ppermute(value, ("xh", "xl"), [(i, i ^ flip) for i in range(4)]) for flip in (2, 3, 1)
    )
    same = jnp.where(xl == 0, jnp.stack([value, near]), jnp.stack([near, value]))
    cross = jnp.where(xl == 0, jnp.stack([far, across]), jnp.stack([across, far]))
    return jnp.where(xh == 0, jnp.stack([same, cross]), jnp.stack([cross, same]))


def with_other_core(pieces):
    return pieces + [lax.ppermute(piece, "core", SWAP) for piece in pieces]


def around(value, axis):
    count = lax.axis_size(axis)
    return [value] + [
        lax.ppermute(value, axis, [(i, (i + k) % count) for i in range(count)])
        for k in range(1, count)
    ]


def body(hidden_states, proj_weight, bilinear, lengths, labels):
    xh, z, y, core = (lax.axis_index(axis) for axis in ("xh", "z", "y", "core"))
    place = jnp.stack([xh, z, y, core])
    lengths = lengths[0]
    rows = proj_weight.shape[0]
    w = gather_core(jnp.concatenate([proj_weight, bilinear], axis=0))
    w = w.reshape(2, -1, w.shape[1])
    w, bil = (v.reshape(-1, v.shape[2]) for v in (w[:, :rows], w[:, rows:]))
    bil = around(bil, "z")
    rows = w.shape[0]
    w = jnp.concatenate([w] + bil, axis=0)
    h = pack(hidden_states[0, 0])
    h, w = lax.optimization_barrier((h, w))
    w = gather_x(w)
    bil = w[:, :, rows:].reshape(2, 2, len(bil), -1, w.shape[3])
    w = with_other_core(around(w[:, :, :rows], "y"))
    h = lax.all_to_all(h, "z", 0, 0)
    parts = (project(place, h, w) * SCALE).astype(jnp.float16)
    parts, bil = lax.optimization_barrier((parts, bil))
    bil = around(bil, "y")
    parts = lax.all_to_all(parts, CAND, 0, 0)
    parts = parts.reshape((2, -1) + parts.shape[1:]).astype(F32)
    x = (jnp.sum(parts, axis=1) * (1.0 / SCALE)).astype(BF).reshape(CANDS * ROWS, SLICE)
    xt, means, col, stat = forward(lengths, x)
    bil, means = lax.optimization_barrier((bil, means))
    bil = with_other_core(bil)
    means = lax.all_to_all(means, CAND, 0, 0)
    far, means = lax.optimization_barrier((h, means))
    far = lax.ppermute(far, "xh", SWAP)
    drows, logits, term = backward(lengths, place, means, bil, x, xt, col, stat, labels)
    drows = lax.all_to_all(drows, "z", 0, 0)
    term = term.reshape(-1, bilinear.shape[0], term.shape[1])
    mine, other = gradient(place, h, far, drows, term)
    other = lax.ppermute(other, "core", SWAP)
    sent = (mine + other.astype(F32)).astype(BF)
    got = lax.all_to_all(sent, ("xh", "xl", "y"), 0, 0)
    grad_proj, grad_bil = finish(got, proj_weight.shape[0], bilinear.shape[0])
    return logits[None], grad_proj, grad_bil


def solution(mesh):
    parts = Mesh(mesh.devices.reshape(2, 4, 2, 4, 2), ("xh", "z", "xl", "y", "core"))
    in_specs = (
        P(PROMPT, CAND, None, None),
        P(CAND + PROMPT, None),
        P(CAND + PROMPT, None),
        P(PROMPT, None),
        P(PROMPT, None),
    )
    out_specs = (P(PROMPT, None, None), P(CAND + PROMPT, None), P(CAND + PROMPT, None))
    return jax.shard_map(body, mesh=parts, in_specs=in_specs, out_specs=out_specs, check_vma=False)
```

```python
import jax
import jax.numpy as jnp
from jax import lax
from jax.experimental import pallas as pl
from jax.experimental.pallas import tpu as pltpu
from jax.sharding import Mesh
from jax.sharding import PartitionSpec as P

HEAD_DIM = 64
CANDS = 8
ROWS = 128
SLICE = 128
WIDTH = 1024
PAIRS = CANDS * CANDS
EPSILON = 1e-06
FAR = 1e30
SCALE = 64.0
HIGH = lax.Precision.HIGHEST
BF = jnp.bfloat16
F32 = jnp.float32
NT = (((1,), (1,)), ((), ()))
NN = (((1,), (0,)), ((), ()))
TN = (((0,), (0,)), ((), ()))
CAND = ("xh", "z")
PROMPT = ("xl", "y", "core")


def mm(left, right, dims=NN, precision=None):
    return lax.dot_general(left, right, dims, precision=precision, preferred_element_type=F32)


def split(value):
    high = value.astype(BF)
    return high, (value - high.astype(F32)).astype(BF)


def lanes(shape):
    return lax.broadcasted_iota(jnp.int32, shape, len(shape) - 1)


def sublanes(shape):
    return lax.broadcasted_iota(jnp.int32, shape, len(shape) - 2)


def pack_kernel(low_ref, high_ref, out_ref):
    half = low_ref.shape[1]
    out_ref[0, :, :half] = low_ref[...]
    out_ref[0, :, half:] = high_ref[...]


def pack(hidden):
    quarter = CANDS // 2
    half = hidden.shape[1] // CANDS
    hidden = pltpu.with_memory_space_constraint(hidden, pltpu.HBM)
    return pl.pallas_call(
        pack_kernel,
        out_shape=jax.ShapeDtypeStruct((quarter, ROWS, 2 * half), BF),
        grid=(quarter,),
        in_specs=[
            pl.BlockSpec((ROWS, half), lambda q: (0, q)),
            pl.BlockSpec((ROWS, half), lambda q: (0, q + CANDS // 2)),
        ],
        out_specs=pl.BlockSpec((1, ROWS, 2 * half), lambda q: (q, 0, 0)),
        compiler_params=pltpu.CompilerParams(vmem_limit_bytes=16 << 20),
    )(hidden, hidden)


def project_kernel(place_ref, h_ref, *refs):
    pieces, (out_ref, w_scr) = refs[:-2], refs[-2:]
    count = len(pieces) // 2
    half = pieces[0].shape[3]

    @pl.when(pl.program_id(0) == 0)
    def _():
        for k in range(count):
            source = lax.rem(place_ref[2] + count - k, count)
            for piece, side in ((pieces[k], place_ref[3]), (pieces[count + k], 1 - place_ref[3])):
                columns = pl.ds(pl.multiple_of(side * half, half), half)
                w_scr[:, :, source, :, columns] = piece[...]

    h = h_ref[...].reshape(h_ref.shape[0] * ROWS, h_ref.shape[2])
    total = mm(h, w_scr[...].reshape(h.shape[1], -1))
    for dest in range(out_ref.shape[0]):
        out_ref[dest] = total[:, dest * SLICE : (dest + 1) * SLICE]


def project(place, h, pieces):
    steps = 2
    per = h.shape[0] // steps
    shape = pieces[0].shape
    depth = h.shape[2]
    count = len(pieces) // 2
    width = 2 * shape[3]
    dests = width // SLICE
    return pl.pallas_call(
        project_kernel,
        out_shape=jax.ShapeDtypeStruct((dests, h.shape[0] * ROWS, SLICE), F32),
        grid=(steps,),
        in_specs=[
            pl.BlockSpec(memory_space=pltpu.SMEM),
            pl.BlockSpec((per, ROWS, depth), lambda s: (s, 0, 0)),
        ]
        + [pl.BlockSpec(shape, lambda s: (0, 0, 0, 0))] * len(pieces),
        out_specs=pl.BlockSpec((dests, per * ROWS, SLICE), lambda s: (0, s, 0)),
        scratch_shapes=[pltpu.VMEM(shape[:2] + (count, shape[2], width), BF)],
        compiler_params=pltpu.CompilerParams(vmem_limit_bytes=32 << 20),
    )(place, h, *pieces)


def extend(x, len_ref):
    blocks = []
    for j in range(CANDS):
        shape = (ROWS, SLICE)
        lane = lanes(shape)
        member = jnp.logical_and(lane < 3 * CANDS, jnp.bitwise_and(lane, CANDS - 1) == j)
        dead = jnp.logical_and(lane == 3 * CANDS, sublanes(shape) >= len_ref[j])
        blocks.append(jnp.where(dead, -FAR, jnp.where(member, 1.0, 0.0)).astype(BF))
    return jnp.concatenate([x, jnp.concatenate(blocks, axis=0)], axis=1)


def head_weights(xt_ref, i, shift=None):
    columns = xt_ref[:, i * ROWS : (i + 1) * ROWS] * jnp.asarray(HEAD_DIM**-0.5, BF)
    zero = jnp.zeros((HEAD_DIM, ROWS), BF)
    top = jnp.concatenate([columns[:HEAD_DIM], zero], axis=1)
    bottom = jnp.concatenate([zero, columns[HEAD_DIM:]], axis=1)
    wide = 2 * ROWS
    if shift is None:
        parts = [jnp.zeros((3 * CANDS, wide), F32)]
    else:
        high = shift.astype(BF).astype(F32)
        rest = shift - high
        middle = rest.astype(BF).astype(F32)
        parts = [-high, -middle, middle - rest]
    parts.append(jnp.where(sublanes((CANDS, wide)) == 0, 1.0, 0.0))
    extra = jnp.concatenate(parts, axis=0).astype(BF)
    return jnp.concatenate([top, bottom, extra, jnp.zeros((SLICE - 4 * CANDS, wide), BF)], axis=0)


def forward_kernel(
    len_ref, x_ref, xt_ref, mean_ref, col_ref, stat_ref, e_scr, m_scr, l_scr, key_scr
):
    x = x_ref[...]
    key_scr[...] = extend(x, len_ref)
    xt_ref[...] = x.T
    wide = 2 * ROWS
    for i in range(CANDS):
        weights = head_weights(xt_ref, i)
        for j in range(CANDS):
            s = mm(key_scr[j * ROWS : (j + 1) * ROWS, :], weights)
            m = jnp.max(s, axis=0, keepdims=True)
            e = jnp.exp(s - m)
            e_scr[i, j * ROWS : (j + 1) * ROWS, :] = e.astype(BF)
            m_scr[i, j : j + 1, :] = m
            l_scr[i, j : j + 1, :] = jnp.sum(e, axis=0, keepdims=True)
    for i in range(CANDS):
        own = len_ref[i]
        shape = (CANDS, wide)
        token = jnp.bitwise_and(lanes(shape), ROWS - 1)
        live = jnp.logical_and(token < own, sublanes(shape) != i)
        weight = 1.0 / own.astype(F32)
        denom = l_scr[i]
        stat_ref[i * CANDS : (i + 1) * CANDS, :] = jnp.where(
            live, m_scr[i] + jnp.log(denom) - jnp.log(weight * HEAD_DIM**-0.5), FAR
        )
        r = jnp.where(live, weight / denom, 0.0)
        first = lanes(shape) < ROWS
        r0h, r0l = split(jnp.where(first, r, 0.0))
        r1h, r1l = split(jnp.where(first, 0.0, r))
        got = mm(jnp.concatenate([r0h, r0l, r1h, r1l], axis=0), e_scr[i], NT)
        block = lanes((CANDS, CANDS * ROWS)) // ROWS == sublanes((CANDS, CANDS * ROWS))
        c0 = jnp.where(block, got[0:8] + got[8:16], 0.0)
        c1 = jnp.where(block, got[16:24] + got[24:32], 0.0)
        col_ref[0, i : i + 1, :] = jnp.sum(c0, axis=0, keepdims=True)
        col_ref[1, i : i + 1, :] = jnp.sum(c1, axis=0, keepdims=True)
        c0h, c0l = split(c0)
        c1h, c1l = split(c1)
        means = mm(jnp.concatenate([c0h, c0l, c1h, c1l], axis=0), x_ref[...])
        means = jnp.where(
            lanes((CANDS, SLICE)) < HEAD_DIM, means[0:8] + means[8:16], means[16:24] + means[24:32]
        )
        for dest in range(CANDS):
            mean_ref[dest, i * CANDS : (i + 1) * CANDS, :] = means


def forward(lengths, x):
    rows = CANDS * ROWS
    vmem = pl.BlockSpec(memory_space=pltpu.VMEM)
    return pl.pallas_call(
        forward_kernel,
        out_shape=(
            jax.ShapeDtypeStruct((SLICE, rows), BF),
            jax.ShapeDtypeStruct((CANDS, PAIRS, SLICE), F32),
            jax.ShapeDtypeStruct((2, CANDS, rows), F32),
            jax.ShapeDtypeStruct((PAIRS, 2 * ROWS), F32),
        ),
        in_specs=[pl.BlockSpec(memory_space=pltpu.SMEM), vmem],
        out_specs=(vmem,) * 4,
        scratch_shapes=[
            pltpu.VMEM((CANDS, rows, 2 * ROWS), BF),
            pltpu.VMEM((CANDS, CANDS, 2 * ROWS), F32),
            pltpu.VMEM((CANDS, CANDS, 2 * ROWS), F32),
            pltpu.VMEM((rows, 2 * SLICE), BF),
        ],
        cost_estimate=pl.CostEstimate(flops=12 << 30, bytes_accessed=16 << 20, transcendentals=2 << 20),
        compiler_params=pltpu.CompilerParams(vmem_limit_bytes=24 << 20),
    )(lengths, x)


def backward_kernel(len_ref, place_ref, mean_ref, x_ref, xt_ref, col_ref, stat_ref, label_ref, *refs):
    bil_refs, refs = refs[:CANDS], refs[CANDS:]
    dr_ref, logit_ref, term_ref, d_scr, along_scr, grad_scr, key_scr, bil_scr = refs
    xh, z, y, core = place_ref[0], place_ref[1], place_ref[2], place_ref[3]
    count, half = len(bil_refs) // 2, WIDTH // 2
    for k in range(count):
        for piece, side in ((bil_refs[k], core), (bil_refs[count + k], 1 - core)):
            columns = pl.ds(pl.multiple_of(side * half, half), half)
            for hi, lo in ((0, 0), (0, 1), (1, 0), (1, 1)):
                for back in range(piece.shape[2]):
                    level = lax.rem(z + piece.shape[2] - back, piece.shape[2])
                    bil_scr[hi, level, lo, lax.rem(y + count - k, count), :, columns] = piece[hi, lo, back]
    key_scr[...] = extend(x_ref[...], len_ref)
    here = xh * (CANDS // 2) + z
    means = jnp.concatenate([mean_ref[c] for c in range(CANDS)], axis=1)
    radius = jnp.sqrt(jnp.mean(means * means, axis=1, keepdims=True) + EPSILON)
    pooled = means / radius
    row, lane = sublanes((PAIRS, PAIRS)), lanes((PAIRS, PAIRS))
    swap = jnp.where(
        jnp.logical_and(row // CANDS == lane % CANDS, row % CANDS == lane // CANDS), 1.0, 0.0
    )
    reverse = mm(swap, pooled, precision=HIGH)
    rev_high, rev_low = split(reverse)
    both = mm(jnp.concatenate([rev_high, rev_low], axis=0), bil_scr[...].reshape(WIDTH, WIDTH), NT)
    toward = both[:PAIRS] + both[PAIRS:]
    logit = jnp.sum(pooled * toward, axis=1, keepdims=True)
    index = sublanes((PAIRS, 1))
    off = index // CANDS != index % CANDS
    logit = jnp.where(off, logit, 0.0)
    labels = label_ref[...]
    shape = (PAIRS, labels.shape[1])
    left, right = sublanes(shape) // CANDS, sublanes(shape) % CANDS
    low, high = jnp.minimum(left, right), jnp.maximum(left, right)
    spot = low * (2 * CANDS - 1 - low) // 2 + high - low - 1
    wins = (2.0 * labels.astype(F32) - 1.0) * jnp.where(left < right, 1.0, -1.0)
    sign = jnp.sum(jnp.where(spot == lanes(shape), wins, 0.0), axis=1, keepdims=True)
    dlogit = jnp.where(off, -sign * jax.nn.sigmoid(-sign * logit), 0.0)
    pick = lanes((PAIRS, SLICE))
    swapped = mm(
        swap, jnp.where(pick == 0, dlogit, jnp.where(pick == 1, logit, 0.0)), precision=HIGH
    )
    dlogit_rev, logit_rev = swapped[:, 0:1], swapped[:, 1:2]
    spread = jnp.where(
        lanes((PAIRS, CANDS)) == sublanes((PAIRS, CANDS)) % CANDS, logit, 0.0
    )
    gather = jnp.where(
        sublanes((CANDS, PAIRS)) == lanes((CANDS, PAIRS)) // CANDS, 1.0, 0.0
    )
    logit_ref[...] = mm(gather, spread, precision=HIGH)
    columns = pl.ds(pl.multiple_of(here * SLICE, SLICE), SLICE)
    back = mm(
        jnp.concatenate([rev_high, rev_low], axis=0),
        bil_scr[:, :, :, :, :, columns].reshape(WIDTH, SLICE),
    )
    back = back[:PAIRS] + back[PAIRS:]
    own_pooled = mean_ref[here] / radius
    own_toward = jnp.zeros((PAIRS, SLICE), F32)
    for c in range(CANDS):
        own_toward += jnp.where(here == c, toward[:, c * SLICE : (c + 1) * SLICE], 0.0)
    dpooled = dlogit * own_toward + dlogit_rev * back
    inner = (dlogit * logit + dlogit_rev * logit_rev) * (1.0 / WIDTH)
    dmeans = (dpooled - own_pooled * inner) / radius
    low_rows = jnp.concatenate(
        [mean_ref[z] / radius, mean_ref[z + CANDS // 2] / radius], axis=1
    ) * dlogit
    rev_half = jnp.where(xh == 0, reverse[:, :half], reverse[:, half:])
    ah, al = split(low_rows)
    bh, bl = split(rev_half)
    term_ref[...] = mm(
        jnp.concatenate([ah, al, ah], axis=0), jnp.concatenate([bh, bh, bl], axis=0), TN
    )
    dmeans_rev = mm(swap, dmeans, precision=HIGH)
    lane8 = lanes((CANDS, SLICE))
    col = col_ref[...].reshape(2 * CANDS, CANDS * ROWS)
    col_high = col.astype(BF).astype(F32)
    turned = jnp.concatenate([col_high, col - col_high, col_high], axis=0).T.astype(BF)
    for j in range(CANDS):
        rows = slice(j * ROWS, (j + 1) * ROWS)
        x = x_ref[rows, :]
        of_j = dmeans_rev[j * CANDS : (j + 1) * CANDS]
        heads = jnp.concatenate(
            [jnp.where(lane8 < HEAD_DIM, of_j, 0.0), jnp.where(lane8 < HEAD_DIM, 0.0, of_j)], axis=0
        )
        hh, hl = split(heads)
        along = mm(
            jnp.concatenate([x, x], axis=1),
            jnp.concatenate(
                [jnp.concatenate([hh, hl], axis=1), jnp.concatenate([hh, hl], axis=1)], axis=0
            ),
            NT,
        )
        ah, al = split(along)
        along_scr[rows, :] = jnp.where(lanes(along.shape) < 2 * CANDS, ah, al)
        grad_scr[rows, :] = mm(turned[rows, :], jnp.concatenate([hh, hh, hl], axis=0))
    wide = 2 * ROWS
    for i in range(CANDS):
        weights = head_weights(xt_ref, i, stat_ref[i * CANDS : (i + 1) * CANDS, :])
        scale = len_ref[i].astype(F32) * HEAD_DIM**0.5
        shape = (4 * CANDS, wide)
        which = jnp.bitwise_and(sublanes(shape), 2 * CANDS - 1)
        chosen = jnp.where(
            which == jnp.where(lanes(shape) < ROWS, i, i + CANDS), 1.0, 0.0
        ).astype(BF)
        for j in range(CANDS):
            rows = slice(j * ROWS, (j + 1) * ROWS)
            p = jnp.exp(mm(key_scr[rows, :], weights))
            along = mm(along_scr[rows, :], chosen)
            expected = jnp.sum(p * along, axis=0, keepdims=True) * scale
            d_scr[i, rows, :] = (p * (along - expected)).astype(BF)
        lane = lanes((ROWS, SLICE))
        own = x_ref[i * ROWS : (i + 1) * ROWS, :]
        zero = jnp.zeros_like(own)
        heads = jnp.concatenate(
            [jnp.where(lane < HEAD_DIM, own, zero), jnp.where(lane < HEAD_DIM, zero, own)], axis=0
        )
        grad_scr[...] += mm(d_scr[i], heads)
        query = mm(xt_ref[...], d_scr[i])
        query = jnp.concatenate([query[:HEAD_DIM, :ROWS], query[HEAD_DIM:, ROWS:]], axis=0)
        grad_scr[i * ROWS : (i + 1) * ROWS, :] += query.T
    drows = grad_scr[...].astype(BF)
    for dest in range(dr_ref.shape[0]):
        dr_ref[dest] = drows


def backward(lengths, place, means, bil, x, xt, col, stat, labels):
    rows = CANDS * ROWS
    vmem = pl.BlockSpec(memory_space=pltpu.VMEM)
    smem = pl.BlockSpec(memory_space=pltpu.SMEM)
    return pl.pallas_call(
        backward_kernel,
        out_shape=(
            jax.ShapeDtypeStruct((CANDS // 2, rows, SLICE), BF),
            jax.ShapeDtypeStruct((CANDS, CANDS), F32),
            jax.ShapeDtypeStruct((2 * SLICE, WIDTH // 2), F32),
        ),
        in_specs=[smem, smem] + [vmem] * (6 + len(bil)),
        out_specs=(vmem,) * 3,
        scratch_shapes=[
            pltpu.VMEM((CANDS, rows, 2 * ROWS), BF),
            pltpu.VMEM((rows, 4 * CANDS), BF),
            pltpu.VMEM((rows, SLICE), F32),
            pltpu.VMEM((rows, 2 * SLICE), BF),
            pltpu.VMEM((2, CANDS // 2, 2, len(bil) // 2, 2 * CANDS, WIDTH), BF),
        ],
        cost_estimate=pl.CostEstimate(flops=8 << 30, bytes_accessed=8 << 20, transcendentals=2 << 20),
        compiler_params=pltpu.CompilerParams(vmem_limit_bytes=32 << 20),
    )(lengths, place, means, x, xt, col, stat, labels, *bil)


def gradient_kernel(place_ref, h_ref, far_ref, d_ref, term_ref, mine_ref, other_ref, d_scr, scr):
    count, rows, depth = h_ref.shape
    groups, block, width = mine_ref.shape
    rows *= count

    @pl.when(pl.program_id(0) == 0)
    def _():
        for part, side in ((0, place_ref[0]), (1, 1 - place_ref[0])):
            source = pl.ds(pl.multiple_of(side * rows, rows), rows)
            for q in range(d_ref.shape[0]):
                d_scr[part * rows : (part + 1) * rows, q * SLICE : (q + 1) * SLICE] = d_ref[q, source, :]

    h = jnp.concatenate([h_ref[...].reshape(rows, depth), far_ref[...].reshape(rows, depth)], axis=0)
    total = mm(h, d_scr[...], TN).reshape(2 * groups, -1, width)
    total = jnp.concatenate([total, term_ref[...]], axis=1)
    scr[...] = total.reshape(groups, 2, block, width)
    core = place_ref[3]
    mine_ref[...] = scr[:, core]
    other_ref[...] = scr[:, 1 - core].astype(BF)


def gradient(place, h, far, d, term):
    count, _, depth = h.shape
    steps = 4
    dests = term.shape[0] // 2
    width = d.shape[0] * d.shape[2]
    block = depth // dests // 2 + term.shape[1]
    groups = dests // steps
    out = pl.BlockSpec((groups, block, width), lambda s: (s, 0, 0))
    hidden = pl.BlockSpec((count, ROWS, depth // steps), lambda s: (0, 0, s))
    return pl.pallas_call(
        gradient_kernel,
        out_shape=(
            jax.ShapeDtypeStruct((dests, block, width), F32),
            jax.ShapeDtypeStruct((dests, block, width), BF),
        ),
        grid=(steps,),
        in_specs=[
            pl.BlockSpec(memory_space=pltpu.SMEM),
            hidden,
            hidden,
            pl.BlockSpec(d.shape, lambda s: (0, 0, 0)),
            pl.BlockSpec((2 * groups,) + term.shape[1:], lambda s: (s, 0, 0)),
        ],
        out_specs=(out, out),
        scratch_shapes=[
            pltpu.VMEM((d.shape[1], width), BF),
            pltpu.VMEM((groups, 2, block, width), F32),
        ],
        compiler_params=pltpu.CompilerParams(vmem_limit_bytes=24 << 20),
    )(place, h, far, d, term)


def finish_kernel(got_ref, proj_ref, bil_ref):
    half = got_ref.shape[2]
    count = got_ref.shape[0] // 2
    for part in range(2):
        total = got_ref[part * count].astype(F32)
        for source in range(1, count):
            total += got_ref[part * count + source].astype(F32)
        columns = slice(part * half, (part + 1) * half)
        proj_ref[:, columns] = total[: proj_ref.shape[0]]
        bil_ref[:, columns] = total[proj_ref.shape[0] :]


def finish(got, rows, bil_rows):
    vmem = pl.BlockSpec(memory_space=pltpu.VMEM)
    width = 2 * got.shape[2]
    return pl.pallas_call(
        finish_kernel,
        out_shape=(
            jax.ShapeDtypeStruct((rows, width), F32),
            jax.ShapeDtypeStruct((bil_rows, width), F32),
        ),
        in_specs=[vmem],
        out_specs=(vmem, vmem),
        compiler_params=pltpu.CompilerParams(vmem_limit_bytes=16 << 20),
    )(got)


SWAP = [(0, 1), (1, 0)]


def gather_core(value):
    first = lax.axis_index("core") == 0
    half = value.shape[-1] // 2
    keep = jnp.where(first, value[..., :half], value[..., half:])
    away = jnp.where(first, value[..., half:], value[..., :half])
    other = lax.ppermute(away, "core", SWAP)
    return jnp.concatenate(
        [jnp.where(first, keep, other), jnp.where(first, other, keep)], axis=-2
    )


def gather_x(value):
    xh, xl = lax.axis_index("xh"), lax.axis_index("xl")
    far, across, near = (
        lax.ppermute(value, ("xh", "xl"), [(i, i ^ flip) for i in range(4)]) for flip in (2, 3, 1)
    )
    same = jnp.where(xl == 0, jnp.stack([value, near]), jnp.stack([near, value]))
    cross = jnp.where(xl == 0, jnp.stack([far, across]), jnp.stack([across, far]))
    return jnp.where(xh == 0, jnp.stack([same, cross]), jnp.stack([cross, same]))


def with_other_core(pieces):
    return pieces + [lax.ppermute(piece, "core", SWAP) for piece in pieces]


def around(value, axis):
    count = lax.axis_size(axis)
    return [value] + [
        lax.ppermute(value, axis, [(i, (i + k) % count) for i in range(count)])
        for k in range(1, count)
    ]


def body(hidden_states, proj_weight, bilinear, lengths, labels):
    xh, z, y, core = (lax.axis_index(axis) for axis in ("xh", "z", "y", "core"))
    place = jnp.stack([xh, z, y, core])
    lengths = lengths[0]
    rows = proj_weight.shape[0]
    w = gather_core(jnp.concatenate([proj_weight, bilinear], axis=0))
    w = w.reshape(2, -1, w.shape[1])
    w, bil = (v.reshape(-1, v.shape[2]) for v in (w[:, :rows], w[:, rows:]))
    w = gather_x(w)
    bil = jnp.stack(around(bil, "z"))
    h = pack(hidden_states[0, 0])
    h, bil = lax.optimization_barrier((h, bil))
    w = with_other_core(around(w, "y"))
    bil = gather_x(bil)
    h = lax.all_to_all(h, "z", 0, 0)
    parts = (project(place, h, w) * SCALE).astype(jnp.float16)
    parts, bil = lax.optimization_barrier((parts, bil))
    bil = around(bil, "y")
    parts = lax.all_to_all(parts, CAND, 0, 0)
    parts = parts.reshape((2, -1) + parts.shape[1:]).astype(F32)
    x = (jnp.sum(parts, axis=1) * (1.0 / SCALE)).astype(BF).reshape(CANDS * ROWS, SLICE)
    xt, means, col, stat = forward(lengths, x)
    bil, means = lax.optimization_barrier((bil, means))
    bil = with_other_core(bil)
    means = lax.all_to_all(means, CAND, 0, 0)
    far, means = lax.optimization_barrier((h, means))
    far = lax.ppermute(far, "xh", SWAP)
    drows, logits, term = backward(lengths, place, means, bil, x, xt, col, stat, labels)
    drows = lax.all_to_all(drows, "z", 0, 0)
    term = term.reshape(-1, bilinear.shape[0], term.shape[1])
    mine, other = gradient(place, h, far, drows, term)
    other = lax.ppermute(other, "core", SWAP)
    sent = (mine + other.astype(F32)).astype(BF)
    got = lax.all_to_all(sent, ("xh", "xl", "y"), 0, 0)
    grad_proj, grad_bil = finish(got, proj_weight.shape[0], bilinear.shape[0])
    return logits[None], grad_proj, grad_bil


def solution(mesh):
    parts = Mesh(mesh.devices.reshape(2, 4, 2, 4, 2), ("xh", "z", "xl", "y", "core"))
    in_specs = (
        P(PROMPT, CAND, None, None),
        P(CAND + PROMPT, None),
        P(CAND + PROMPT, None),
        P(PROMPT, None),
        P(PROMPT, None),
    )
    out_specs = (P(PROMPT, None, None), P(CAND + PROMPT, None), P(CAND + PROMPT, None))
    return jax.shard_map(body, mesh=parts, in_specs=in_specs, out_specs=out_specs, check_vma=False)
```

```python
import jax
import jax.numpy as jnp
from jax import lax
from jax.experimental import pallas as pl
from jax.experimental.pallas import tpu as pltpu
from jax.sharding import Mesh
from jax.sharding import PartitionSpec as P

HEAD_DIM = 64
CANDS = 8
ROWS = 128
SLICE = 128
WIDTH = 1024
PAIRS = CANDS * CANDS
EPSILON = 1e-06
FAR = 1e30
SCALE = 64.0
HIGH = lax.Precision.HIGHEST
BF = jnp.bfloat16
F32 = jnp.float32
NT = (((1,), (1,)), ((), ()))
NN = (((1,), (0,)), ((), ()))
TN = (((0,), (0,)), ((), ()))
CAND = ("xh", "z")
PROMPT = ("xl", "y", "core")


def mm(left, right, dims=NN, precision=None):
    return lax.dot_general(left, right, dims, precision=precision, preferred_element_type=F32)


def split(value):
    high = value.astype(BF)
    return high, (value - high.astype(F32)).astype(BF)


def lanes(shape):
    return lax.broadcasted_iota(jnp.int32, shape, len(shape) - 1)


def sublanes(shape):
    return lax.broadcasted_iota(jnp.int32, shape, len(shape) - 2)


def pack_kernel(low_ref, high_ref, out_ref):
    half = low_ref.shape[1]
    out_ref[0, :, :half] = low_ref[...]
    out_ref[0, :, half:] = high_ref[...]


def pack(hidden):
    quarter = CANDS // 2
    half = hidden.shape[1] // CANDS
    hidden = pltpu.with_memory_space_constraint(hidden, pltpu.HBM)
    return pl.pallas_call(
        pack_kernel,
        out_shape=jax.ShapeDtypeStruct((quarter, ROWS, 2 * half), BF),
        grid=(quarter,),
        in_specs=[
            pl.BlockSpec((ROWS, half), lambda q: (0, q)),
            pl.BlockSpec((ROWS, half), lambda q: (0, q + CANDS // 2)),
        ],
        out_specs=pl.BlockSpec((1, ROWS, 2 * half), lambda q: (q, 0, 0)),
        compiler_params=pltpu.CompilerParams(vmem_limit_bytes=16 << 20),
    )(hidden, hidden)


def project_kernel(place_ref, h_ref, *refs):
    pieces, (out_ref, w_scr) = refs[:-2], refs[-2:]
    count = len(pieces) // 2
    half = pieces[0].shape[3]

    @pl.when(pl.program_id(0) == 0)
    def _():
        for k in range(count):
            source = lax.rem(place_ref[2] + count - k, count)
            for piece, side in ((pieces[k], place_ref[3]), (pieces[count + k], 1 - place_ref[3])):
                columns = pl.ds(pl.multiple_of(side * half, half), half)
                w_scr[:, :, source, :, columns] = piece[...]

    h = h_ref[...].reshape(h_ref.shape[0] * ROWS, h_ref.shape[2])
    total = mm(h, w_scr[...].reshape(h.shape[1], -1))
    for dest in range(out_ref.shape[0]):
        out_ref[dest] = total[:, dest * SLICE : (dest + 1) * SLICE]


def project(place, h, pieces):
    steps = 2
    per = h.shape[0] // steps
    shape = pieces[0].shape
    depth = h.shape[2]
    count = len(pieces) // 2
    width = 2 * shape[3]
    dests = width // SLICE
    return pl.pallas_call(
        project_kernel,
        out_shape=jax.ShapeDtypeStruct((dests, h.shape[0] * ROWS, SLICE), F32),
        grid=(steps,),
        in_specs=[
            pl.BlockSpec(memory_space=pltpu.SMEM),
            pl.BlockSpec((per, ROWS, depth), lambda s: (s, 0, 0)),
        ]
        + [pl.BlockSpec(shape, lambda s: (0, 0, 0, 0))] * len(pieces),
        out_specs=pl.BlockSpec((dests, per * ROWS, SLICE), lambda s: (0, s, 0)),
        scratch_shapes=[pltpu.VMEM(shape[:2] + (count, shape[2], width), BF)],
        compiler_params=pltpu.CompilerParams(vmem_limit_bytes=32 << 20),
    )(place, h, *pieces)


def extend(x, len_ref):
    blocks = []
    for j in range(CANDS):
        shape = (ROWS, SLICE)
        lane = lanes(shape)
        member = jnp.logical_and(lane < 3 * CANDS, jnp.bitwise_and(lane, CANDS - 1) == j)
        dead = jnp.logical_and(lane == 3 * CANDS, sublanes(shape) >= len_ref[j])
        blocks.append(jnp.where(dead, -FAR, jnp.where(member, 1.0, 0.0)).astype(BF))
    return jnp.concatenate([x, jnp.concatenate(blocks, axis=0)], axis=1)


def head_weights(xt_ref, i, shift=None):
    columns = xt_ref[:, i * ROWS : (i + 1) * ROWS] * jnp.asarray(HEAD_DIM**-0.5, BF)
    zero = jnp.zeros((HEAD_DIM, ROWS), BF)
    top = jnp.concatenate([columns[:HEAD_DIM], zero], axis=1)
    bottom = jnp.concatenate([zero, columns[HEAD_DIM:]], axis=1)
    wide = 2 * ROWS
    if shift is None:
        parts = [jnp.zeros((3 * CANDS, wide), F32)]
    else:
        high = shift.astype(BF).astype(F32)
        rest = shift - high
        middle = rest.astype(BF).astype(F32)
        parts = [-high, -middle, middle - rest]
    parts.append(jnp.where(sublanes((CANDS, wide)) == 0, 1.0, 0.0))
    extra = jnp.concatenate(parts, axis=0).astype(BF)
    return jnp.concatenate([top, bottom, extra, jnp.zeros((SLICE - 4 * CANDS, wide), BF)], axis=0)


def forward_kernel(
    len_ref, x_ref, xt_ref, mean_ref, col_ref, stat_ref, e_scr, m_scr, l_scr, key_scr
):
    x = x_ref[...]
    key_scr[...] = extend(x, len_ref)
    xt_ref[...] = x.T
    wide = 2 * ROWS
    for i in range(CANDS):
        weights = head_weights(xt_ref, i)
        for j in range(CANDS):
            s = mm(key_scr[j * ROWS : (j + 1) * ROWS, :], weights)
            m = jnp.max(s, axis=0, keepdims=True)
            e = jnp.exp(s - m)
            e_scr[i, j * ROWS : (j + 1) * ROWS, :] = e.astype(BF)
            m_scr[i, j : j + 1, :] = m
            l_scr[i, j : j + 1, :] = jnp.sum(e, axis=0, keepdims=True)
    for i in range(CANDS):
        own = len_ref[i]
        shape = (CANDS, wide)
        token = jnp.bitwise_and(lanes(shape), ROWS - 1)
        live = jnp.logical_and(token < own, sublanes(shape) != i)
        weight = 1.0 / own.astype(F32)
        denom = l_scr[i]
        stat_ref[i * CANDS : (i + 1) * CANDS, :] = jnp.where(
            live, m_scr[i] + jnp.log(denom) - jnp.log(weight * HEAD_DIM**-0.5), FAR
        )
        r = jnp.where(live, weight / denom, 0.0)
        first = lanes(shape) < ROWS
        r0h, r0l = split(jnp.where(first, r, 0.0))
        r1h, r1l = split(jnp.where(first, 0.0, r))
        got = mm(jnp.concatenate([r0h, r0l, r1h, r1l], axis=0), e_scr[i], NT)
        block = lanes((CANDS, CANDS * ROWS)) // ROWS == sublanes((CANDS, CANDS * ROWS))
        c0 = jnp.where(block, got[0:8] + got[8:16], 0.0)
        c1 = jnp.where(block, got[16:24] + got[24:32], 0.0)
        col_ref[0, i : i + 1, :] = jnp.sum(c0, axis=0, keepdims=True)
        col_ref[1, i : i + 1, :] = jnp.sum(c1, axis=0, keepdims=True)
        c0h, c0l = split(c0)
        c1h, c1l = split(c1)
        means = mm(jnp.concatenate([c0h, c0l, c1h, c1l], axis=0), x_ref[...])
        means = jnp.where(
            lanes((CANDS, SLICE)) < HEAD_DIM, means[0:8] + means[8:16], means[16:24] + means[24:32]
        )
        for dest in range(CANDS):
            mean_ref[dest, i * CANDS : (i + 1) * CANDS, :] = means


def forward(lengths, x):
    rows = CANDS * ROWS
    vmem = pl.BlockSpec(memory_space=pltpu.VMEM)
    return pl.pallas_call(
        forward_kernel,
        out_shape=(
            jax.ShapeDtypeStruct((SLICE, rows), BF),
            jax.ShapeDtypeStruct((CANDS, PAIRS, SLICE), F32),
            jax.ShapeDtypeStruct((2, CANDS, rows), F32),
            jax.ShapeDtypeStruct((PAIRS, 2 * ROWS), F32),
        ),
        in_specs=[pl.BlockSpec(memory_space=pltpu.SMEM), vmem],
        out_specs=(vmem,) * 4,
        scratch_shapes=[
            pltpu.VMEM((CANDS, rows, 2 * ROWS), BF),
            pltpu.VMEM((CANDS, CANDS, 2 * ROWS), F32),
            pltpu.VMEM((CANDS, CANDS, 2 * ROWS), F32),
            pltpu.VMEM((rows, 2 * SLICE), BF),
        ],
        cost_estimate=pl.CostEstimate(flops=12 << 30, bytes_accessed=16 << 20, transcendentals=2 << 20),
        compiler_params=pltpu.CompilerParams(vmem_limit_bytes=24 << 20),
    )(lengths, x)


def backward_kernel(len_ref, place_ref, mean_ref, x_ref, xt_ref, col_ref, stat_ref, label_ref, *refs):
    bil_refs, refs = refs[:CANDS], refs[CANDS:]
    dr_ref, logit_ref, term_ref, d_scr, along_scr, grad_scr, key_scr, bil_scr = refs
    xh, z, y, core = place_ref[0], place_ref[1], place_ref[2], place_ref[3]
    count, half = len(bil_refs) // 2, WIDTH // 2
    for k in range(count):
        for piece, side in ((bil_refs[k], core), (bil_refs[count + k], 1 - core)):
            columns = pl.ds(pl.multiple_of(side * half, half), half)
            for hi, lo in ((0, 0), (0, 1), (1, 0), (1, 1)):
                for back in range(piece.shape[2]):
                    level = lax.rem(z + piece.shape[2] - back, piece.shape[2])
                    bil_scr[hi, level, lo, lax.rem(y + count - k, count), :, columns] = piece[hi, lo, back]
    key_scr[...] = extend(x_ref[...], len_ref)
    here = xh * (CANDS // 2) + z
    means = jnp.concatenate([mean_ref[c] for c in range(CANDS)], axis=1)
    radius = jnp.sqrt(jnp.mean(means * means, axis=1, keepdims=True) + EPSILON)
    pooled = means / radius
    row, lane = sublanes((PAIRS, PAIRS)), lanes((PAIRS, PAIRS))
    swap = jnp.where(
        jnp.logical_and(row // CANDS == lane % CANDS, row % CANDS == lane // CANDS), 1.0, 0.0
    )
    reverse = mm(swap, pooled, precision=HIGH)
    rev_high, rev_low = split(reverse)
    both = mm(jnp.concatenate([rev_high, rev_low], axis=0), bil_scr[...].reshape(WIDTH, WIDTH), NT)
    toward = both[:PAIRS] + both[PAIRS:]
    logit = jnp.sum(pooled * toward, axis=1, keepdims=True)
    index = sublanes((PAIRS, 1))
    off = index // CANDS != index % CANDS
    logit = jnp.where(off, logit, 0.0)
    labels = label_ref[...]
    shape = (PAIRS, labels.shape[1])
    left, right = sublanes(shape) // CANDS, sublanes(shape) % CANDS
    low, high = jnp.minimum(left, right), jnp.maximum(left, right)
    spot = low * (2 * CANDS - 1 - low) // 2 + high - low - 1
    wins = (2.0 * labels.astype(F32) - 1.0) * jnp.where(left < right, 1.0, -1.0)
    sign = jnp.sum(jnp.where(spot == lanes(shape), wins, 0.0), axis=1, keepdims=True)
    dlogit = jnp.where(off, -sign * jax.nn.sigmoid(-sign * logit), 0.0)
    pick = lanes((PAIRS, SLICE))
    swapped = mm(
        swap, jnp.where(pick == 0, dlogit, jnp.where(pick == 1, logit, 0.0)), precision=HIGH
    )
    dlogit_rev, logit_rev = swapped[:, 0:1], swapped[:, 1:2]
    spread = jnp.where(
        lanes((PAIRS, CANDS)) == sublanes((PAIRS, CANDS)) % CANDS, logit, 0.0
    )
    gather = jnp.where(
        sublanes((CANDS, PAIRS)) == lanes((CANDS, PAIRS)) // CANDS, 1.0, 0.0
    )
    logit_ref[...] = mm(gather, spread, precision=HIGH)
    columns = pl.ds(pl.multiple_of(here * SLICE, SLICE), SLICE)
    back = mm(
        jnp.concatenate([rev_high, rev_low], axis=0),
        bil_scr[:, :, :, :, :, columns].reshape(WIDTH, SLICE),
    )
    back = back[:PAIRS] + back[PAIRS:]
    own_pooled = mean_ref[here] / radius
    own_toward = jnp.zeros((PAIRS, SLICE), F32)
    for c in range(CANDS):
        own_toward += jnp.where(here == c, toward[:, c * SLICE : (c + 1) * SLICE], 0.0)
    dpooled = dlogit * own_toward + dlogit_rev * back
    inner = (dlogit * logit + dlogit_rev * logit_rev) * (1.0 / WIDTH)
    dmeans = (dpooled - own_pooled * inner) / radius
    low_rows = jnp.concatenate(
        [mean_ref[z] / radius, mean_ref[z + CANDS // 2] / radius], axis=1
    ) * dlogit
    rev_half = jnp.where(xh == 0, reverse[:, :half], reverse[:, half:])
    ah, al = split(low_rows)
    bh, bl = split(rev_half)
    term_ref[...] = mm(
        jnp.concatenate([ah, al, ah], axis=0), jnp.concatenate([bh, bh, bl], axis=0), TN
    )
    dmeans_rev = mm(swap, dmeans, precision=HIGH)
    lane8 = lanes((CANDS, SLICE))
    col = col_ref[...].reshape(2 * CANDS, CANDS * ROWS)
    col_high = col.astype(BF).astype(F32)
    turned = jnp.concatenate([col_high, col - col_high, col_high], axis=0).T.astype(BF)
    for j in range(CANDS):
        rows = slice(j * ROWS, (j + 1) * ROWS)
        x = x_ref[rows, :]
        of_j = dmeans_rev[j * CANDS : (j + 1) * CANDS]
        heads = jnp.concatenate(
            [jnp.where(lane8 < HEAD_DIM, of_j, 0.0), jnp.where(lane8 < HEAD_DIM, 0.0, of_j)], axis=0
        )
        hh, hl = split(heads)
        along = mm(
            jnp.concatenate([x, x], axis=1),
            jnp.concatenate(
                [jnp.concatenate([hh, hl], axis=1), jnp.concatenate([hh, hl], axis=1)], axis=0
            ),
            NT,
        )
        ah, al = split(along)
        along_scr[rows, :] = jnp.where(lanes(along.shape) < 2 * CANDS, ah, al)
        grad_scr[rows, :] = mm(turned[rows, :], jnp.concatenate([hh, hh, hl], axis=0))
    wide = 2 * ROWS
    for i in range(CANDS):
        weights = head_weights(xt_ref, i, stat_ref[i * CANDS : (i + 1) * CANDS, :])
        scale = len_ref[i].astype(F32) * HEAD_DIM**0.5
        shape = (4 * CANDS, wide)
        which = jnp.bitwise_and(sublanes(shape), 2 * CANDS - 1)
        chosen = jnp.where(
            which == jnp.where(lanes(shape) < ROWS, i, i + CANDS), 1.0, 0.0
        ).astype(BF)
        for j in range(CANDS):
            rows = slice(j * ROWS, (j + 1) * ROWS)
            p = jnp.exp(mm(key_scr[rows, :], weights))
            along = mm(along_scr[rows, :], chosen)
            expected = jnp.sum(p * along, axis=0, keepdims=True) * scale
            d_scr[i, rows, :] = (p * (along - expected)).astype(BF)
        lane = lanes((ROWS, SLICE))
        own = x_ref[i * ROWS : (i + 1) * ROWS, :]
        zero = jnp.zeros_like(own)
        heads = jnp.concatenate(
            [jnp.where(lane < HEAD_DIM, own, zero), jnp.where(lane < HEAD_DIM, zero, own)], axis=0
        )
        grad_scr[...] += mm(d_scr[i], heads)
        query = mm(xt_ref[...], d_scr[i])
        query = jnp.concatenate([query[:HEAD_DIM, :ROWS], query[HEAD_DIM:, ROWS:]], axis=0)
        grad_scr[i * ROWS : (i + 1) * ROWS, :] += query.T
    drows = grad_scr[...].astype(BF)
    for dest in range(dr_ref.shape[0]):
        dr_ref[dest] = drows


def backward(lengths, place, means, bil, x, xt, col, stat, labels):
    rows = CANDS * ROWS
    vmem = pl.BlockSpec(memory_space=pltpu.VMEM)
    smem = pl.BlockSpec(memory_space=pltpu.SMEM)
    return pl.pallas_call(
        backward_kernel,
        out_shape=(
            jax.ShapeDtypeStruct((CANDS // 2, rows, SLICE), BF),
            jax.ShapeDtypeStruct((CANDS, CANDS), F32),
            jax.ShapeDtypeStruct((2 * SLICE, WIDTH // 2), F32),
        ),
        in_specs=[smem, smem] + [vmem] * (6 + len(bil)),
        out_specs=(vmem,) * 3,
        scratch_shapes=[
            pltpu.VMEM((CANDS, rows, 2 * ROWS), BF),
            pltpu.VMEM((rows, 4 * CANDS), BF),
            pltpu.VMEM((rows, SLICE), F32),
            pltpu.VMEM((rows, 2 * SLICE), BF),
            pltpu.VMEM((2, CANDS // 2, 2, len(bil) // 2, 2 * CANDS, WIDTH), BF),
        ],
        cost_estimate=pl.CostEstimate(flops=8 << 30, bytes_accessed=8 << 20, transcendentals=2 << 20),
        compiler_params=pltpu.CompilerParams(vmem_limit_bytes=32 << 20),
    )(lengths, place, means, x, xt, col, stat, labels, *bil)


def gradient_kernel(place_ref, h_ref, far_ref, d_ref, term_ref, mine_ref, other_ref, d_scr, scr):
    count, rows, depth = h_ref.shape
    groups, block, width = mine_ref.shape
    rows *= count

    @pl.when(pl.program_id(0) == 0)
    def _():
        for part, side in ((0, place_ref[0]), (1, 1 - place_ref[0])):
            source = pl.ds(pl.multiple_of(side * rows, rows), rows)
            for q in range(d_ref.shape[0]):
                d_scr[part * rows : (part + 1) * rows, q * SLICE : (q + 1) * SLICE] = d_ref[q, source, :]

    h = jnp.concatenate([h_ref[...].reshape(rows, depth), far_ref[...].reshape(rows, depth)], axis=0)
    total = mm(h, d_scr[...], TN).reshape(2 * groups, -1, width)
    total = jnp.concatenate([total, term_ref[...]], axis=1)
    scr[...] = total.reshape(groups, 2, block, width)
    core = place_ref[3]
    mine_ref[...] = scr[:, core]
    other_ref[...] = scr[:, 1 - core].astype(BF)


def gradient(place, h, far, d, term):
    count, _, depth = h.shape
    steps = 4
    dests = term.shape[0] // 2
    width = d.shape[0] * d.shape[2]
    block = depth // dests // 2 + term.shape[1]
    groups = dests // steps
    out = pl.BlockSpec((groups, block, width), lambda s: (s, 0, 0))
    hidden = pl.BlockSpec((count, ROWS, depth // steps), lambda s: (0, 0, s))
    return pl.pallas_call(
        gradient_kernel,
        out_shape=(
            jax.ShapeDtypeStruct((dests, block, width), F32),
            jax.ShapeDtypeStruct((dests, block, width), BF),
        ),
        grid=(steps,),
        in_specs=[
            pl.BlockSpec(memory_space=pltpu.SMEM),
            hidden,
            hidden,
            pl.BlockSpec(d.shape, lambda s: (0, 0, 0)),
            pl.BlockSpec((2 * groups,) + term.shape[1:], lambda s: (s, 0, 0)),
        ],
        out_specs=(out, out),
        scratch_shapes=[
            pltpu.VMEM((d.shape[1], width), BF),
            pltpu.VMEM((groups, 2, block, width), F32),
        ],
        compiler_params=pltpu.CompilerParams(vmem_limit_bytes=24 << 20),
    )(place, h, far, d, term)


def finish_kernel(got_ref, proj_ref, bil_ref):
    half = got_ref.shape[2]
    count = got_ref.shape[0] // 2
    for part in range(2):
        total = got_ref[part * count].astype(F32)
        for source in range(1, count):
            total += got_ref[part * count + source].astype(F32)
        columns = slice(part * half, (part + 1) * half)
        proj_ref[:, columns] = total[: proj_ref.shape[0]]
        bil_ref[:, columns] = total[proj_ref.shape[0] :]


def finish(got, rows, bil_rows):
    vmem = pl.BlockSpec(memory_space=pltpu.VMEM)
    width = 2 * got.shape[2]
    return pl.pallas_call(
        finish_kernel,
        out_shape=(
            jax.ShapeDtypeStruct((rows, width), F32),
            jax.ShapeDtypeStruct((bil_rows, width), F32),
        ),
        in_specs=[vmem],
        out_specs=(vmem, vmem),
        compiler_params=pltpu.CompilerParams(vmem_limit_bytes=16 << 20),
    )(got)


SWAP = [(0, 1), (1, 0)]


def gather_core(value):
    first = lax.axis_index("core") == 0
    half = value.shape[-1] // 2
    keep = jnp.where(first, value[..., :half], value[..., half:])
    away = jnp.where(first, value[..., half:], value[..., :half])
    other = lax.ppermute(away, "core", SWAP)
    return jnp.concatenate(
        [jnp.where(first, keep, other), jnp.where(first, other, keep)], axis=-2
    )


def gather_x(value):
    xh, xl = lax.axis_index("xh"), lax.axis_index("xl")
    far, across, near = (
        lax.ppermute(value, ("xh", "xl"), [(i, i ^ flip) for i in range(4)]) for flip in (2, 3, 1)
    )
    same = jnp.where(xl == 0, jnp.stack([value, near]), jnp.stack([near, value]))
    cross = jnp.where(xl == 0, jnp.stack([far, across]), jnp.stack([across, far]))
    return jnp.where(xh == 0, jnp.stack([same, cross]), jnp.stack([cross, same]))


def with_other_core(pieces):
    return pieces + [lax.ppermute(piece, "core", SWAP) for piece in pieces]


def around(value, axis):
    count = lax.axis_size(axis)
    return [value] + [
        lax.ppermute(value, axis, [(i, (i + k) % count) for i in range(count)])
        for k in range(1, count)
    ]


def body(hidden_states, proj_weight, bilinear, lengths, labels):
    xh, z, y, core = (lax.axis_index(axis) for axis in ("xh", "z", "y", "core"))
    place = jnp.stack([xh, z, y, core])
    lengths = lengths[0]
    rows = proj_weight.shape[0]
    w = gather_core(jnp.concatenate([proj_weight, bilinear], axis=0))
    w = w.reshape(2, -1, w.shape[1])
    w, bil = (v.reshape(-1, v.shape[2]) for v in (w[:, :rows], w[:, rows:]))
    w = gather_x(w)
    h = pack(hidden_states[0, 0])
    h, bil = lax.optimization_barrier((h, bil))
    bil = jnp.stack(around(bil, "z"))
    h, bil = lax.optimization_barrier((h, bil))
    w = with_other_core(around(w, "y"))
    bil = gather_x(bil)
    h = lax.all_to_all(h, "z", 0, 0)
    parts = (project(place, h, w) * SCALE).astype(jnp.float16)
    parts, bil = lax.optimization_barrier((parts, bil))
    bil = around(bil, "y")
    parts = lax.all_to_all(parts, CAND, 0, 0)
    parts = parts.reshape((2, -1) + parts.shape[1:]).astype(F32)
    x = (jnp.sum(parts, axis=1) * (1.0 / SCALE)).astype(BF).reshape(CANDS * ROWS, SLICE)
    xt, means, col, stat = forward(lengths, x)
    bil, means = lax.optimization_barrier((bil, means))
    bil = with_other_core(bil)
    means = lax.all_to_all(means, CAND, 0, 0)
    far, means = lax.optimization_barrier((h, means))
    far = lax.ppermute(far, "xh", SWAP)
    drows, logits, term = backward(lengths, place, means, bil, x, xt, col, stat, labels)
    drows = lax.all_to_all(drows, "z", 0, 0)
    term = term.reshape(-1, bilinear.shape[0], term.shape[1])
    mine, other = gradient(place, h, far, drows, term)
    other = lax.ppermute(other, "core", SWAP)
    sent = (mine + other.astype(F32)).astype(BF)
    got = lax.all_to_all(sent, ("xh", "xl", "y"), 0, 0)
    grad_proj, grad_bil = finish(got, proj_weight.shape[0], bilinear.shape[0])
    return logits[None], grad_proj, grad_bil


def solution(mesh):
    parts = Mesh(mesh.devices.reshape(2, 4, 2, 4, 2), ("xh", "z", "xl", "y", "core"))
    in_specs = (
        P(PROMPT, CAND, None, None),
        P(CAND + PROMPT, None),
        P(CAND + PROMPT, None),
        P(PROMPT, None),
        P(PROMPT, None),
    )
    out_specs = (P(PROMPT, None, None), P(CAND + PROMPT, None), P(CAND + PROMPT, None))
    return jax.shard_map(body, mesh=parts, in_specs=in_specs, out_specs=out_specs, check_vma=False)
```
